256 devices in a mesh: freq: 64 (over x, z, y_lo), rec: 4 (over y_hi, core).
Axes of the slice: x: 4, y: 4 (y_hi: 2, y_lo: 2; y = y_hi * 2 + y_lo), z: 8, core: 2. Of those that a mesh axis runs over, the one named last changes fastest.
Arguments:
- response: bfloat16 [2, 256, 768, 3072], P(None, 'freq', None, 'rec'), may hold values from -0.078125 to 0.078125
- focus_init: bfloat16 [3072, 256, 128], P('rec', 'freq'), may hold values from -6 to 6
- onset_src: int32 [768, 64], replicated, may hold values from 80 to 639
- onset_rec: int32 [3072, 64], P('rec'), may hold values from 80 to 639
Outputs:
- focus_minus: float32 [768, 256, 128], P('rec', 'freq')
- focus_plus: float32 [3072, 256, 128], P('rec', 'freq')
The draws below stay inside these ranges and needn't reach their ends.
All inputs are finite; a program needn't handle non-finite values.
Results may differ from the reference program's by a relative error of at most 0.0022.
Values may be sent and summed in bfloat16 or wider, within the bound.
No kernel may reach another device: no remote copies, remote signals or barrier semaphores. Data moves between devices by JAX's collectives and lax.ppermute only.
A program may use at most 64 MiB of HBM per device.

```python
import math
import jax
import jax.numpy as jnp
from jax import lax

S = 768
REC = 3072
F = 256
NT = 640
P_SIZE = 64
ITERS = 2


def plant(result, key, smallest, high):
    shape = result.shape
    spot = [jax.random.randint(jax.random.fold_in(key, axis), (), 0, shape[axis]) for axis in range(len(shape))]
    result = result.at[tuple(spot)].set(smallest)
    longest = shape.index(max(shape))
    spot[longest] = (spot[longest] + 1) % shape[longest]
    return result.at[tuple(spot)].set(high)


def block_levels(key, dims, cuts, least, high):
    def one(axis_at, blocks):
        steps = jax.random.uniform(jax.random.fold_in(jax.random.fold_in(key, 6), axis_at), (blocks,), jnp.float32, least / len(cuts), high / len(cuts))
        return jnp.repeat(jnp.exp(steps), dims[axis_at] // blocks).reshape((-1,) + (1,) * (len(dims) - axis_at - 1))

    loudness = one(*cuts[0])
    for cut in cuts[1:]:
        loudness = loudness * one(*cut)
    return loudness


def noise(stream_key, dims, scale, most, cuts=(), kind=jnp.bfloat16):
    factor_of = block_levels(stream_key, dims, cuts, -0.22, 0.18) if cuts else 1.0
    result = jax.random.normal(stream_key, dims, jnp.float32) * scale * factor_of
    return jnp.minimum(jnp.maximum(result, -most), most).astype(kind)


def setup_inputs(seed: int = 0) -> dict:
    key_list = jax.random.split(jax.random.key(seed), 5)
    return {
        "response": noise(key_list[0], (2, F, S, REC), (2 * REC) ** -0.5, 0.078125, ((1, 64), (3, 4))),
        "focus_init": noise(key_list[1], (REC, F, 2 * P_SIZE), 1.0, 6.0, ((0, 4), (1, 64))),
        "onset_src": plant(jax.random.randint(key_list[2], (S, P_SIZE), NT // 8, NT), jax.random.fold_in(key_list[2], 1), NT // 8, NT - 1).astype(jnp.int32),
        "onset_rec": plant(jax.random.randint(key_list[3], (REC, P_SIZE), NT // 8, NT), jax.random.fold_in(key_list[3], 1), NT // 8, NT - 1).astype(jnp.int32),
    }


def tables():
    bins = jnp.arange(F, dtype=jnp.int32) + 1
    samples = jnp.arange(NT, dtype=jnp.int32)
    phase_idx = (bins[:, None] * samples[None, :]) % NT
    angles = phase_idx.astype(jnp.float32) * (2.0 * math.pi / NT)
    cosine = jnp.cos(angles)
    sine = jnp.sin(angles)
    inverse = jnp.stack([cosine, -sine], axis=1) * (2.0 / NT)
    forward = jnp.stack([cosine, -sine], axis=1)
    return inverse, forward


def window(values, onsets, inverse, forward):
    rows = values.shape[0]
    split = values.reshape(rows, F, 2, P_SIZE)
    traces = jnp.einsum("rkcp,kcn->rpn", split, inverse, precision=lax.Precision.HIGHEST)
    keep = jnp.arange(NT, dtype=jnp.int32)[None, None, :] < onsets[:, :, None]
    traces = jnp.where(keep, traces, jnp.zeros_like(traces))
    back = jnp.einsum("rpn,kcn->rkcp", traces, forward, precision=lax.Precision.HIGHEST)
    return back.reshape(rows, F, 2 * P_SIZE)


def apply_response(response, plus_bf):
    def one_bin(k):
        slab = response[:, k].astype(jnp.float32)
        field = plus_bf[:, k, :].astype(jnp.float32)
        first = jnp.dot(slab[0], field, precision=lax.Precision.HIGHEST, preferred_element_type=jnp.float32)
        second = jnp.dot(slab[1], field, precision=lax.Precision.HIGHEST, preferred_element_type=jnp.float32)
        real_part = first[:, :P_SIZE] - second[:, P_SIZE:]
        imag_part = first[:, P_SIZE:] + second[:, :P_SIZE]
        return jnp.concatenate([real_part, imag_part], axis=1)

    stacked = lax.map(one_bin, jnp.arange(F, dtype=jnp.int32))
    return jnp.transpose(stacked, (1, 0, 2))


def apply_adjoint(response, minus_bf):
    def one_bin(k):
        slab = response[:, k].astype(jnp.float32)
        field = minus_bf[:, k, :].astype(jnp.float32)
        first = jnp.dot(slab[0].T, field, precision=lax.Precision.HIGHEST, preferred_element_type=jnp.float32)
        second = jnp.dot(slab[1].T, field, precision=lax.Precision.HIGHEST, preferred_element_type=jnp.float32)
        real_part = first[:, :P_SIZE] + second[:, P_SIZE:]
        imag_part = first[:, P_SIZE:] - second[:, :P_SIZE]
        return jnp.concatenate([real_part, imag_part], axis=1)

    stacked = lax.map(one_bin, jnp.arange(F, dtype=jnp.int32))
    return jnp.transpose(stacked, (1, 0, 2))


def reference(response, focus_init, onset_src, onset_rec):
    inverse, forward = tables()
    plus_bf = focus_init
    minus = None
    plus = None
    for step in range(ITERS):
        ahead = apply_response(response, plus_bf)
        minus = window(ahead, onset_src, inverse, forward)
        minus_bf = minus.astype(jnp.bfloat16)
        behind = apply_adjoint(response, minus_bf)
        plus = focus_init.astype(jnp.float32) + window(behind, onset_rec, inverse, forward)
        plus_bf = plus.astype(jnp.bfloat16)
    return minus, plus
```

```python
import math

import jax
import jax.numpy as jnp
import numpy as np
from jax import lax
from jax.experimental import pallas as pl
from jax.experimental.pallas import tpu as pltpu
from jax.sharding import PartitionSpec as P

NT = 640
ITERS = 2
HALF = 64
R_ABS = 0.078125 * math.sqrt(2.0) * 1.001
TOP = 16384.0
FLOOR = 2.0 ** -14
HIGH = lax.Precision.HIGH


def trig_table(nbins):
    bins = np.arange(nbins, dtype=np.int64) + 1
    samples = np.arange(NT, dtype=np.int64)
    phase = (bins[:, None] * samples[None, :]) % NT
    angles = phase.astype(np.float64) * (2.0 * math.pi / NT)
    both = np.stack([np.cos(angles), -np.sin(angles)], axis=1)
    return both.reshape(2 * nbins, NT).astype(np.float32)


def forward_kernel(order_ref, a_ref, b_ref, x_ref, o_ref):
    x = x_ref[0]
    half = x.shape[1] // 2
    y = jnp.concatenate([-x[:, half:], x[:, :half]], axis=1)
    for i, part in enumerate((a_ref, b_ref)):
        o_ref[i, 0] = jnp.dot(part[0, 0], x, preferred_element_type=jnp.float32) + jnp.dot(
            part[1, 0], y, preferred_element_type=jnp.float32
        )


def forward_call(response, plus, order):
    _, bins, sources, recs = response.shape
    width = plus.shape[2]
    block = sources // 4
    return pl.pallas_call(
        forward_kernel,
        grid_spec=pltpu.PrefetchScalarGridSpec(
            num_scalar_prefetch=1,
            grid=(bins,),
            in_specs=[
                pl.BlockSpec((2, 1, block, recs), lambda k, o: (0, k, o[0], 0)),
                pl.BlockSpec((2, 1, block, recs), lambda k, o: (0, k, o[1], 0)),
                pl.BlockSpec((1, recs, width), lambda k, o: (k, 0, 0)),
            ],
            out_specs=pl.BlockSpec((2, 1, block, width), lambda k, o: (0, k, 0, 0)),
        ),
        out_shape=jax.ShapeDtypeStruct((2, bins, block, width), jnp.float32),
        cost_estimate=pl.CostEstimate(
            flops=2 * bins * sources * recs * width, bytes_accessed=bins * sources * recs * 2, transcendentals=0
        ),
    )(order, response, response, plus)


def adjoint_kernel(r_ref, m_ref, o_ref):
    m = m_ref[:, 0]
    m = m.reshape(m.shape[0] * m.shape[1], m.shape[2])
    half = m.shape[1] // 2
    n = jnp.concatenate([m[:, half:], -m[:, :half]], axis=1)
    dims = (((0,), (0,)), ((), ()))
    o_ref[0] = lax.dot_general(m, r_ref[0, 0], dims, preferred_element_type=jnp.float32) + lax.dot_general(
        n, r_ref[1, 0], dims, preferred_element_type=jnp.float32
    )


def adjoint_call(response, minus):
    _, bins, sources, recs = response.shape
    width = minus.shape[3]
    return pl.pallas_call(
        adjoint_kernel,
        grid=(bins,),
        in_specs=[
            pl.BlockSpec((2, 1, sources, recs), lambda k: (0, k, 0, 0)),
            pl.BlockSpec((4, 1, sources // 4, width), lambda k: (0, k, 0, 0)),
        ],
        out_specs=pl.BlockSpec((1, width, recs), lambda k: (k, 0, 0)),
        out_shape=jax.ShapeDtypeStruct((bins, width, recs), jnp.float32),
        cost_estimate=pl.CostEstimate(
            flops=4 * bins * sources * recs * width, bytes_accessed=bins * sources * recs * 4, transcendentals=0
        ),
    )(response, minus)


def window(x, onsets, inverse_t, forward):
    traces = jnp.dot(inverse_t, x, precision=HIGH, preferred_element_type=jnp.float32)
    keep = lax.broadcasted_iota(jnp.int32, traces.shape, 0) < onsets[None, :]
    traces = jnp.where(keep, traces, 0.0)
    return jnp.dot(forward, traces, precision=HIGH, preferred_element_type=jnp.float32)


def body(response, focus_init, onset_src, onset_rec):
    nfreq = lax.axis_size("freq")
    freq_pos = lax.axis_index("freq")
    rec_pos = lax.axis_index("rec")
    _, bins, sources, recs = response.shape
    width = focus_init.shape[2]
    block = sources // 4
    rows = block // nfreq
    used = rows * bins
    spare = -used % 16 + (16 if used % 16 == 0 else 0)
    core, high = rec_pos % 2, rec_pos // 2

    table = trig_table(bins * nfreq)
    forward = jnp.asarray(table)
    inverse_t = jnp.asarray(np.ascontiguousarray((table * np.float32(2.0 / NT)).T))

    rec_onsets = lax.dynamic_slice_in_dim(onset_rec.T, freq_pos, 1, 0)[0]
    src_onsets = lax.dynamic_slice_in_dim(onset_src, rec_pos * block + freq_pos * rows, rows, 0).reshape(-1)

    def swap(values):
        return lax.all_to_all(values, "freq", split_axis=0, concat_axis=0, tiled=True)

    init_k = jnp.transpose(focus_init, (1, 0, 2))
    peak_init = jnp.maximum(jnp.max(jnp.abs(focus_init)).astype(jnp.float32), FLOOR)
    init_norm = math.sqrt(2.0 * bins * nfreq)
    rec_gain = 4 * recs * R_ABS
    src_gain = sources * R_ABS

    send_order = jnp.stack([(1 - high) * 2 + 1 - core, high * 2 + 1 - core]).astype(jnp.int32)
    keep_order = jnp.stack([(1 - high) * 2 + core, high * 2 + core]).astype(jnp.int32)

    plus = init_k
    ahead_bound = rec_gain * init_norm * 6.0
    minus_out = None
    plus_out = None
    for step in range(ITERS):
        last = step == ITERS - 1
        ahead_scale = TOP / ahead_bound
        sent = forward_call(response, plus, send_order)
        other = lax.ppermute(sent, "rec", [(0, 1), (1, 0), (2, 3), (3, 2)])
        kept = forward_call(response, plus, keep_order)
        kept = kept + other
        coded = (kept[0] * ahead_scale).astype(jnp.float16)
        far = lax.ppermute(coded, "rec", [(0, 2), (2, 0), (1, 3), (3, 1)])
        ahead = kept[1] * ahead_scale + far.astype(jnp.float32)
        ahead = jnp.transpose(ahead.reshape(bins, nfreq, rows, width), (1, 2, 0, 3)).reshape(nfreq, used, width)
        first_spare = jnp.full((nfreq, spare, width), peak_init, jnp.float32)
        ahead = jnp.concatenate([ahead, first_spare], axis=1).astype(jnp.float16)
        field = swap(ahead)
        peak = jnp.max(field[:, used:, :]).astype(jnp.float32)
        field = field[:, :used].reshape(nfreq, rows, bins, 2, HALF)
        field = jnp.transpose(field, (0, 2, 3, 1, 4)).reshape(nfreq * bins * 2, rows * HALF).astype(jnp.float32)
        minus = window(field, src_onsets, inverse_t, forward)
        norm = jnp.sqrt(jnp.max(jnp.sum(minus * minus, axis=0)))
        minus = jnp.transpose(minus.reshape(nfreq, bins, 2, rows, HALF), (0, 3, 1, 2, 4)).reshape(nfreq, used, width)
        lane = lax.broadcasted_iota(jnp.int32, (nfreq, spare, width), 2)
        stats = jnp.where(lane < HALF, norm * 1.01, peak)
        minus = swap(jnp.concatenate([minus, stats], axis=1).astype(jnp.float16))
        stats = jnp.max(minus[:, used:, :].astype(jnp.float32), axis=(0, 1))
        minus = minus[:, :used].astype(jnp.float32) * (1.0 / ahead_scale)
        minus = minus.reshape(block, bins, width)
        if last:
            minus_out = minus
        minus_k = jnp.transpose(minus, (1, 0, 2))
        stats = jnp.broadcast_to(jnp.maximum(stats, FLOOR) * 1.01, (bins, 16, width))
        gathered = lax.all_gather(
            jnp.concatenate([minus_k, stats], axis=1).astype(jnp.bfloat16), "rec", axis=0, tiled=False
        )
        stats = jnp.max(gathered[:, :, block:, :].astype(jnp.float32), axis=(0, 1, 2))
        norm_bound = jnp.max(stats[:HALF]) * 1.01 / ahead_scale
        peak_bound = jnp.max(stats[HALF:]) * 1.01
        behind_bound = src_gain * norm_bound
        behind_scale = TOP / behind_bound
        behind = adjoint_call(response, gathered[:, :, :block, :])
        behind = jnp.transpose(behind.reshape(2 * bins, HALF, recs), (1, 0, 2))
        field = swap((behind * behind_scale).astype(jnp.float16))
        field = field.reshape(nfreq * bins * 2, recs).astype(jnp.float32)
        back = window(field, rec_onsets, inverse_t, forward)
        back = swap(back.reshape(nfreq, bins * 2, recs).astype(jnp.float16))
        back = back.astype(jnp.float32) * (behind_bound * (1.0 / TOP))
        back = back.reshape(HALF, bins, 2, recs)
        if last:
            back = jnp.transpose(back, (3, 1, 2, 0)).reshape(recs, bins, width)
            plus_out = focus_init.astype(jnp.float32) + back
        else:
            back = jnp.transpose(back, (1, 3, 2, 0)).reshape(bins, recs, width)
            plus = (init_k.astype(jnp.float32) + back).astype(jnp.bfloat16)
            ahead_bound = rec_gain * (init_norm * peak_bound + behind_bound)
    return (minus_out, plus_out)


def solution(mesh):
    return jax.shard_map(
        body,
        mesh=mesh,
        in_specs=(P(None, "freq", None, "rec"), P("rec", "freq", None), P(), P("rec", None)),
        out_specs=(P("rec", "freq", None), P("rec", "freq", None)),
        check_vma=False,
    )
```

```python
import math

import jax
import jax.numpy as jnp
import numpy as np
from jax import lax
from jax.experimental import pallas as pl
from jax.experimental.pallas import tpu as pltpu
from jax.sharding import PartitionSpec as P

NT = 640
ITERS = 2
HALF = 64
FOLD = 336
R_ABS = 0.078125 * math.sqrt(2.0) * 1.001
INIT_ABS = 6.0
TOP = 16384.0
FLOOR = 2.0 ** -14
VMEM_LIMIT = 24 * 1024 * 1024
F32 = jnp.float32
BF16 = jnp.bfloat16
F16 = jnp.float16

CORE_SWAP = [(0, 1), (1, 0), (2, 3), (3, 2)]
HIGH_SWAP = [(0, 2), (2, 0), (1, 3), (3, 1)]


def vmem():
    return pl.BlockSpec(memory_space=pltpu.VMEM)


def smem():
    return pl.BlockSpec(memory_space=pltpu.SMEM)


def call(kernel, out_shape, specs, flops, moved):
    return pl.pallas_call(
        kernel,
        in_specs=specs,
        out_specs=jax.tree.map(lambda _: vmem(), out_shape),
        out_shape=out_shape,
        compiler_params=pltpu.CompilerParams(vmem_limit_bytes=VMEM_LIMIT),
        cost_estimate=pl.CostEstimate(flops=flops, bytes_accessed=moved, transcendentals=0),
    )


def high_low(values):
    values = np.asarray(values, np.float32)
    high = values.astype(jnp.bfloat16)
    return [high, (values - high.astype(np.float32)).astype(jnp.bfloat16)]


def fold_tables(nbins):
    bins = np.arange(nbins, dtype=np.int64) + 1
    samples = np.arange(FOLD, dtype=np.int64)
    angles = ((bins[:, None] * samples[None, :]) % NT).astype(np.float64) * (2.0 * math.pi / NT)
    used = samples[None, :] <= NT // 2
    cosine = np.where(used, np.cos(angles), 0.0)
    sine = np.where(used, np.sin(angles), 0.0)
    forward = np.stack(high_low(cosine) + high_low(sine))
    inverse = np.stack(high_low(cosine.T * (2.0 / NT)) + high_low(sine.T * (2.0 / NT)))
    return forward, inverse


def split_dot(high, low, x):
    x_high = x.astype(BF16)
    x_low = (x - x_high.astype(F32)).astype(BF16)
    total = jnp.dot(high, x_high, preferred_element_type=F32)
    total = total + jnp.dot(high, x_low, preferred_element_type=F32)
    return total + jnp.dot(low, x_high, preferred_element_type=F32)


def window_kernel(with_norm, x_ref, onset_ref, forward_ref, inverse_ref, o_ref):
    blocks, _, lanes = x_ref.shape
    x = x_ref[...].reshape(blocks // 2, 2, 8, lanes)
    even, odd = x[:, 0], x[:, 1]
    first = lax.broadcasted_iota(jnp.int32, even.shape, 1) < 4
    real = jnp.where(first, even, pltpu.roll(odd, 4, 1)).reshape(blocks * 4, lanes)
    imag = jnp.where(first, pltpu.roll(even, 4, 1), odd).reshape(blocks * 4, lanes)
    a = split_dot(inverse_ref[0], inverse_ref[1], real)
    b = split_dot(inverse_ref[2], inverse_ref[3], imag)
    n = lax.broadcasted_iota(jnp.int32, a.shape, 0)
    onset = onset_ref[...]
    near = jnp.where(n < onset, a - b, 0.0)
    far = jnp.where((NT - n < onset) & (n > 0) & (n < NT // 2), a + b, 0.0)
    real = split_dot(forward_ref[0], forward_ref[1], near + far)
    imag = split_dot(forward_ref[2], forward_ref[3], far - near)
    norm = None
    if with_norm:
        norm = jnp.sqrt(jnp.max(jnp.sum(real * real + imag * imag, axis=0, keepdims=True))) * 1.01
    real = real.reshape(blocks // 2, 8, lanes)
    imag = imag.reshape(blocks // 2, 8, lanes)
    even = jnp.where(first, real, pltpu.roll(imag, 4, 1))
    odd = jnp.where(first, pltpu.roll(real, 4, 1), imag)
    if with_norm:
        spare = lax.broadcasted_iota(jnp.int32, even.shape, 2) >= 3 * HALF
        even = jnp.where(spare, norm, even)
        odd = jnp.where(spare, norm, odd)
    o_ref[...] = jnp.concatenate([even[:, None], odd[:, None]], axis=1).reshape(blocks, 8, lanes)


def window_call(x, onsets, tables, with_norm):
    lanes = x.shape[2]
    return call(
        lambda *refs: window_kernel(with_norm, *refs),
        jax.ShapeDtypeStruct(x.shape, F32),
        [vmem()] * 4,
        12 * FOLD * 512 * lanes,
        2 * 4 * x.size,
    )(x, onsets, *tables)


def forward_kernel(picks, order_ref, r_ref, x_ref, o_ref):
    _, bins, block, _ = o_ref.shape
    dims = (((1,), (1,)), ((), ()))
    for k in range(bins):
        x = x_ref[k]
        y = jnp.concatenate([-x[HALF:], x[:HALF]], axis=0)
        starts = [pl.multiple_of(order_ref[pick] * block, HALF) for pick in picks]
        real = jnp.concatenate([r_ref[0, k, pl.ds(at, block), :] for at in starts], axis=0)
        imag = jnp.concatenate([r_ref[1, k, pl.ds(at, block), :] for at in starts], axis=0)
        both = lax.dot_general(real, x, dims, preferred_element_type=F32)
        both = both + lax.dot_general(imag, y, dims, preferred_element_type=F32)
        for i in range(len(picks)):
            o_ref[i, k] = both[i * block : (i + 1) * block]


def forward_call(order, response, plus, picks):
    _, bins, sources, recs = response.shape
    width = plus.shape[1]
    block = sources // 4
    return call(
        lambda *refs: forward_kernel(picks, *refs),
        jax.ShapeDtypeStruct((len(picks), bins, block, width), F32),
        [smem(), vmem(), vmem()],
        4 * bins * len(picks) * block * recs * width,
        4 * bins * len(picks) * block * recs,
    )(order, response, plus)


def adjoint_sum(order_ref, picks, r_ref, parts, k):
    block = r_ref.shape[2] // 4
    m = jnp.concatenate([part[k, :block, :] for part in parts], axis=0).T
    n = jnp.concatenate([m[HALF:], -m[:HALF]], axis=0)
    starts = [pl.multiple_of(order_ref[pick] * block, HALF) for pick in picks]
    real = jnp.concatenate([r_ref[0, k, pl.ds(at, block), :] for at in starts], axis=0)
    imag = jnp.concatenate([r_ref[1, k, pl.ds(at, block), :] for at in starts], axis=0)
    return jnp.dot(m, real, preferred_element_type=F32) + jnp.dot(n, imag, preferred_element_type=F32)


def adjoint_first_kernel(order_ref, r_ref, a_ref, b_ref, o_ref):
    for k in range(r_ref.shape[1]):
        o_ref[k] = adjoint_sum(order_ref, (3, 2), r_ref, (a_ref, b_ref), k)


def adjoint_first(order, response, mine, beside):
    _, bins, sources, recs = response.shape
    width = mine.shape[2]
    return call(
        adjoint_first_kernel,
        jax.ShapeDtypeStruct((bins, width, recs), F32),
        [smem()] + [vmem()] * 3,
        2 * bins * sources * recs * width,
        2 * bins * sources * recs,
    )(order, response, mine, beside)


def adjoint_last_kernel(gain, order_ref, r_ref, total_ref, unit_ref, a_ref, b_ref, c_ref, d_ref, o_ref, bound_ref):
    bins = r_ref.shape[1]
    block = r_ref.shape[2] // 4
    recs = r_ref.shape[3]
    peak = a_ref[0, block:, :]
    for part in (b_ref, c_ref, d_ref):
        peak = jnp.maximum(peak, part[0, block:, :])
    norm = jnp.maximum(jnp.max(peak.astype(F32), axis=0, keepdims=True), FLOOR)
    norm = jnp.broadcast_to(norm * (1.01 * 1.01 * gain), unit_ref.shape) * unit_ref[...]
    bound_ref[...] = norm
    scale = jnp.max(TOP / norm)
    real, imag = [], []
    for k in range(bins):
        both = total_ref[k] + adjoint_sum(order_ref, (1, 0), r_ref, (c_ref, d_ref), k)
        both = both * scale
        real.append(both[:HALF][None])
        imag.append(both[HALF:][None])
    both = jnp.concatenate(real + imag, axis=0)
    o_ref[...] = jnp.transpose(both, (1, 0, 2))


def adjoint_last(order, response, total, unit, parts):
    _, bins, sources, recs = response.shape
    width = total.shape[1]
    gain = sources * R_ABS
    return call(
        lambda *refs: adjoint_last_kernel(gain, *refs),
        (jax.ShapeDtypeStruct((HALF, 2 * bins, recs), F32), jax.ShapeDtypeStruct(unit.shape, F32)),
        [smem()] + [vmem()] * 7,
        2 * bins * sources * recs * width,
        2 * bins * sources * recs,
    )(order, response, total, unit, *parts)


def source_pack_kernel(kept_ref, other_ref, far_ref, scale_ref, o_ref):
    bins, block, width = kept_ref.shape
    scale = scale_ref[0:1, :]
    pieces = {}
    for k in range(bins):
        total = (kept_ref[k] + other_ref[k]) * scale + far_ref[k]
        rows = [total[i * HALF : (i + 1) * HALF] for i in range(3)]
        for c in range(2):
            cut = [row[:, c * HALF : (c + 1) * HALF] for row in rows]
            cut.append(jnp.zeros_like(cut[0]))
            pieces[c, k] = jnp.concatenate(cut, axis=1)[None]
    both = jnp.concatenate([pieces[c, k] for c in range(2) for k in range(bins)], axis=0)
    o_ref[...] = jnp.transpose(both, (1, 0, 2))


def source_pack(kept, other, far, scale):
    bins = kept.shape[0]
    return call(
        source_pack_kernel,
        jax.ShapeDtypeStruct((HALF, 2 * bins, 4 * HALF), F32),
        [vmem()] * 4,
        0,
        16 * kept.size,
    )(kept, other, far, scale)


def source_unpack_kernel(x_ref, unit_ref, o_ref, m_ref):
    bins, block, width = o_ref.shape
    unit = unit_ref[0:1, :]
    both = jnp.transpose(x_ref[...], (1, 0, 2))
    norm = jnp.max(jnp.max(x_ref[:, 0, 3 * HALF :], axis=0, keepdims=True))
    for k in range(bins):
        for i in range(3):
            cut = slice(i * HALF, (i + 1) * HALF)
            rows = jnp.concatenate([both[k][:, cut], both[bins + k][:, cut]], axis=1) * unit
            o_ref[k, cut, :] = rows
            m_ref[k, cut, :] = rows.astype(BF16)
        m_ref[k, block:, :] = jnp.full((16, width), norm, F32).astype(BF16)


def source_unpack(x, unit, bins):
    block, width = 3 * HALF, 2 * HALF
    return call(
        source_unpack_kernel,
        (
            jax.ShapeDtypeStruct((bins, block, width), F32),
            jax.ShapeDtypeStruct((bins, block + 16, width), BF16),
        ),
        [vmem()] * 2,
        0,
        16 * bins * block * width,
    )(x, unit)


def plus_kernel(x_ref, init_ref, unit_ref, o_ref):
    bins, _, recs = init_ref.shape
    unit = jnp.max(unit_ref[...])
    both = jnp.transpose(x_ref[...], (1, 0, 2))
    for k in range(bins):
        rows = jnp.concatenate([both[k], both[bins + k]], axis=0) * unit
        o_ref[k] = (init_ref[k].astype(F32) + rows).astype(BF16)


def plus_call(x, init, unit):
    return call(plus_kernel, jax.ShapeDtypeStruct(init.shape, BF16), [vmem()] * 3, 0, 8 * x.size)(x, init, unit)


def body(response, focus_init, onset_src, onset_rec):
    nfreq = lax.axis_size("freq")
    freq_pos = lax.axis_index("freq")
    rec_pos = lax.axis_index("rec")
    _, bins, sources, recs = response.shape
    width = focus_init.shape[2]
    block = sources // 4
    core, high = rec_pos % 2, rec_pos // 2
    tables = [jnp.asarray(t) for t in fold_tables(bins * nfreq)]

    def place(h, c):
        return h * 2 + c

    order = jnp.stack([place(1 - high, 1 - core), place(1 - high, core), place(high, 1 - core), place(high, core)])
    order = order.astype(jnp.int32)

    rec_onsets = lax.dynamic_slice_in_dim(onset_rec.T, freq_pos, 1, 0)
    rows = rec_pos * block + jnp.arange(3) * HALF + freq_pos
    src_onsets = jnp.concatenate([onset_src[rows].reshape(1, -1), jnp.zeros((1, HALF), jnp.int32)], axis=1)

    def swap(values):
        return lax.all_to_all(values.astype(F16), "freq", split_axis=0, concat_axis=0, tiled=True).astype(F32)

    def step_to(values, pairs):
        return lax.ppermute(values, "rec", pairs)

    init_t = jnp.transpose(focus_init, (1, 2, 0))
    init_norm = math.sqrt(2.0 * bins * nfreq) * INIT_ABS
    rec_gain = 4 * recs * R_ABS

    plus = init_t
    bound = jnp.full((8, 128), rec_gain * init_norm, F32)
    minus_out = None
    plus_out = None
    for step in range(ITERS):
        last = step == ITERS - 1
        scale = TOP / bound
        unit = bound * (1.0 / TOP)
        away = forward_call(order, response, plus, (0,))
        away_other = step_to(away, CORE_SWAP)
        away_mine = forward_call(order, response, plus, (1,))
        coded = ((away_mine + away_other)[0] * scale[0, 0]).astype(F16)
        far = step_to(coded, HIGH_SWAP)
        near = forward_call(order, response, plus, (2, 3))
        near_other = step_to(near[0], CORE_SWAP)
        field = source_pack(near[1], near_other, far.astype(F32), scale)
        field = swap(field)
        field = window_call(field, src_onsets, tables, True)
        minus, mine = source_unpack(swap(field), unit, bins)
        if last:
            minus_out = jnp.transpose(minus, (1, 0, 2))
        beside = step_to(mine, CORE_SWAP)
        across = step_to(mine, HIGH_SWAP)
        total = adjoint_first(order, response, mine, beside)
        corner = step_to(across, CORE_SWAP)
        behind, behind_bound = adjoint_last(order, response, total, unit, (mine, beside, across, corner))
        field = window_call(swap(behind), rec_onsets, tables, False)
        back = swap(field)
        back_unit = behind_bound * (1.0 / TOP)
        if last:
            back = back.reshape(HALF, 2, bins, recs) * back_unit[0, 0]
            back = jnp.transpose(back, (3, 2, 1, 0)).reshape(recs, bins, width)
            plus_out = focus_init.astype(F32) + back
        else:
            plus = plus_call(back, init_t, back_unit)
            bound = rec_gain * (init_norm + behind_bound)
    return (minus_out, plus_out)


def solution(mesh):
    return jax.shard_map(
        body,
        mesh=mesh,
        in_specs=(P(None, "freq", None, "rec"), P("rec", "freq", None), P(), P("rec", None)),
        out_specs=(P("rec", "freq", None), P("rec", "freq", None)),
        check_vma=False,
    )
```

```python
import math

import jax
import jax.numpy as jnp
import numpy as np
from jax import lax
from jax.experimental import pallas as pl
from jax.experimental.pallas import tpu as pltpu
from jax.sharding import PartitionSpec as P

NT = 640
ITERS = 2
HALF = 64
FOLD = 336
R_ABS = 0.078125 * math.sqrt(2.0) * 1.001
INIT_ABS = 6.0
TOP = 16384.0
FLOOR = 2.0 ** -14
MIB = 1024 * 1024
F32 = jnp.float32
BF16 = jnp.bfloat16
F16 = jnp.float16

CORE_SWAP = [(0, 1), (1, 0), (2, 3), (3, 2)]
HIGH_SWAP = [(0, 2), (2, 0), (1, 3), (3, 1)]


def vmem():
    return pl.BlockSpec(memory_space=pltpu.VMEM)


def smem():
    return pl.BlockSpec(memory_space=pltpu.SMEM)


def call(kernel, out_shape, specs, flops, moved, limit=8):
    return pl.pallas_call(
        kernel,
        in_specs=specs,
        out_specs=jax.tree.map(lambda _: vmem(), out_shape),
        out_shape=out_shape,
        compiler_params=pltpu.CompilerParams(vmem_limit_bytes=limit * MIB),
        cost_estimate=pl.CostEstimate(flops=flops, bytes_accessed=moved, transcendentals=0),
    )


def high_low(values):
    values = np.asarray(values, np.float32)
    high = values.astype(jnp.bfloat16)
    return [high, (values - high.astype(np.float32)).astype(jnp.bfloat16)]


def fold_tables(nbins):
    bins = np.arange(nbins, dtype=np.int64) + 1
    samples = np.arange(FOLD, dtype=np.int64)
    angles = ((bins[:, None] * samples[None, :]) % NT).astype(np.float64) * (2.0 * math.pi / NT)
    used = samples[None, :] <= NT // 2
    cosine = np.where(used, np.cos(angles), 0.0)
    sine = np.where(used, np.sin(angles), 0.0)
    forward = np.stack(high_low(cosine) + high_low(sine))
    inverse = np.stack(high_low(cosine.T * (2.0 / NT)) + high_low(sine.T * (2.0 / NT)))
    return forward, inverse


def split_dot(high, low, x):
    x_high = x.astype(BF16)
    x_low = (x - x_high.astype(F32)).astype(BF16)
    total = jnp.dot(high, x_high, preferred_element_type=F32)
    total = total + jnp.dot(high, x_low, preferred_element_type=F32)
    return total + jnp.dot(low, x_high, preferred_element_type=F32)


def window_kernel(with_norm, x_ref, onset_ref, forward_ref, inverse_ref, o_ref):
    blocks, _, lanes = x_ref.shape
    x = x_ref[...].reshape(blocks // 2, 2, 8, lanes)
    even, odd = x[:, 0], x[:, 1]
    first = lax.broadcasted_iota(jnp.int32, even.shape, 1) < 4
    real = jnp.where(first, even, pltpu.roll(odd, 4, 1)).reshape(blocks * 4, lanes)
    imag = jnp.where(first, pltpu.roll(even, 4, 1), odd).reshape(blocks * 4, lanes)
    a = split_dot(inverse_ref[0], inverse_ref[1], real)
    b = split_dot(inverse_ref[2], inverse_ref[3], imag)
    n = lax.broadcasted_iota(jnp.int32, a.shape, 0)
    onset = onset_ref[...]
    near = jnp.where(n < onset, a - b, 0.0)
    far = jnp.where((NT - n < onset) & (n > 0) & (n < NT // 2), a + b, 0.0)
    real = split_dot(forward_ref[0], forward_ref[1], near + far)
    imag = split_dot(forward_ref[2], forward_ref[3], far - near)
    norm = None
    if with_norm:
        norm = jnp.sqrt(jnp.max(jnp.sum(real * real + imag * imag, axis=0, keepdims=True))) * 1.01
    real = real.reshape(blocks // 2, 8, lanes)
    imag = imag.reshape(blocks // 2, 8, lanes)
    even = jnp.where(first, real, pltpu.roll(imag, 4, 1))
    odd = jnp.where(first, pltpu.roll(real, 4, 1), imag)
    if with_norm:
        spare = lax.broadcasted_iota(jnp.int32, even.shape, 2) >= 3 * HALF
        even = jnp.where(spare, norm, even)
        odd = jnp.where(spare, norm, odd)
    o_ref[...] = jnp.concatenate([even[:, None], odd[:, None]], axis=1).reshape(blocks, 8, lanes)


def window_call(x, onsets, tables, with_norm):
    lanes = x.shape[2]
    return call(
        lambda *refs: window_kernel(with_norm, *refs),
        jax.ShapeDtypeStruct(x.shape, F32),
        [vmem()] * 4,
        12 * FOLD * 512 * lanes,
        2 * 4 * x.size,
        16,
    )(x, onsets, *tables)


def forward_bin(picks, order_ref, r_ref, x_ref, o_ref, k):
    block = o_ref.shape[2]
    dims = (((1,), (1,)), ((), ()))
    x = x_ref[k]
    y = jnp.concatenate([-x[HALF:], x[:HALF]], axis=0)
    starts = [pl.multiple_of(order_ref[pick] * block, HALF) for pick in picks]
    real = jnp.concatenate([r_ref[0, k, pl.ds(at, block), :] for at in starts], axis=0)
    imag = jnp.concatenate([r_ref[1, k, pl.ds(at, block), :] for at in starts], axis=0)
    both = lax.dot_general(real, x, dims, preferred_element_type=F32)
    both = both + lax.dot_general(imag, y, dims, preferred_element_type=F32)
    for i in range(len(picks)):
        o_ref[i, k] = both[i * block : (i + 1) * block]


def forward_kernel(picks, order_ref, r_ref, x_ref, o_ref):
    for k in range(o_ref.shape[1]):
        forward_bin(picks, order_ref, r_ref, x_ref, o_ref, k)


def forward_call(order, response, plus, picks):
    _, bins, sources, recs = response.shape
    width = plus.shape[1]
    block = sources // 4
    return call(
        lambda *refs: forward_kernel(picks, *refs),
        jax.ShapeDtypeStruct((len(picks), bins, block, width), F32),
        [smem(), vmem(), vmem()],
        4 * bins * len(picks) * block * recs * width,
        4 * bins * len(picks) * block * recs,
    )(order, response, plus)


def adjoint_sum(order_ref, picks, r_ref, parts, k):
    block = r_ref.shape[2] // 4
    m = jnp.concatenate([part[k * block : (k + 1) * block, :] for part in parts], axis=0).T
    n = jnp.concatenate([m[HALF:], -m[:HALF]], axis=0)
    starts = [pl.multiple_of(order_ref[pick] * block, HALF) for pick in picks]
    real = jnp.concatenate([r_ref[0, k, pl.ds(at, block), :] for at in starts], axis=0)
    imag = jnp.concatenate([r_ref[1, k, pl.ds(at, block), :] for at in starts], axis=0)
    return jnp.dot(m, real, preferred_element_type=F32) + jnp.dot(n, imag, preferred_element_type=F32)


def adjoint_first_kernel(order_ref, r_ref, a_ref, b_ref, o_ref):
    for k in range(r_ref.shape[1]):
        o_ref[k] = adjoint_sum(order_ref, (3, 2), r_ref, (a_ref, b_ref), k)


def adjoint_first(order, response, mine, beside):
    _, bins, sources, recs = response.shape
    width = mine.shape[1]
    return call(
        adjoint_first_kernel,
        jax.ShapeDtypeStruct((bins, width, recs), F32),
        [smem()] + [vmem()] * 3,
        2 * bins * sources * recs * width,
        2 * bins * sources * recs,
    )(order, response, mine, beside)


def adjoint_last_kernel(
    gain,
    rec_gain,
    init_norm,
    order_ref,
    r_ref,
    total_ref,
    unit_ref,
    a_ref,
    b_ref,
    c_ref,
    d_ref,
    o_ref,
    back_ref,
    next_scale_ref,
    next_unit_ref,
):
    bins = r_ref.shape[1]
    block = r_ref.shape[2] // 4
    recs = r_ref.shape[3]
    peak = a_ref[bins * block :, :]
    for part in (b_ref, c_ref, d_ref):
        peak = jnp.maximum(peak, part[bins * block :, :])
    norm = jnp.maximum(jnp.max(peak.astype(F32), axis=0, keepdims=True), FLOOR)
    norm = jnp.broadcast_to(norm * (1.01 * 1.01 * gain), unit_ref.shape) * unit_ref[...]
    back_ref[...] = norm * (1.0 / TOP)
    after = rec_gain * (init_norm + norm)
    next_scale_ref[...] = TOP / after
    next_unit_ref[...] = after * (1.0 / TOP)
    scale = jnp.max(TOP / norm)
    real, imag = [], []
    for k in range(bins):
        both = total_ref[k] + adjoint_sum(order_ref, (1, 0), r_ref, (c_ref, d_ref), k)
        both = both * scale
        real.append(both[:HALF][None])
        imag.append(both[HALF:][None])
    both = jnp.concatenate(real + imag, axis=0)
    o_ref[...] = jnp.transpose(both, (1, 0, 2))


def adjoint_last(order, response, total, unit, parts, rec_gain, init_norm):
    _, bins, sources, recs = response.shape
    width = total.shape[1]
    gain = sources * R_ABS
    stat = jax.ShapeDtypeStruct(unit.shape, F32)
    return call(
        lambda *refs: adjoint_last_kernel(gain, rec_gain, init_norm, *refs),
        (jax.ShapeDtypeStruct((HALF, 2 * bins, recs), F32), stat, stat, stat),
        [smem()] + [vmem()] * 7,
        2 * bins * sources * recs * width,
        2 * bins * sources * recs,
    )(order, response, total, unit, *parts)


def source_pack_kernel(kept_ref, other_ref, far_ref, scale_ref, o_ref):
    _, bins, block, width = kept_ref.shape
    scale = scale_ref[0:1, :]
    pieces = {}
    for k in range(bins):
        total = (kept_ref[0, k] + other_ref[1, k]) * scale + far_ref[k]
        rows = [total[i * HALF : (i + 1) * HALF] for i in range(3)]
        for c in range(2):
            cut = [row[:, c * HALF : (c + 1) * HALF] for row in rows]
            cut.append(jnp.zeros_like(cut[0]))
            pieces[c, k] = jnp.concatenate(cut, axis=1)[None]
    both = jnp.concatenate([pieces[c, k] for c in range(2) for k in range(bins)], axis=0)
    o_ref[...] = jnp.transpose(both, (1, 0, 2))


def source_pack(kept, other, far, scale):
    bins = kept.shape[1]
    return call(
        source_pack_kernel,
        jax.ShapeDtypeStruct((HALF, 2 * bins, 4 * HALF), F32),
        [vmem()] * 4,
        0,
        16 * kept.size,
    )(kept, other, far, scale)


def source_unpack_kernel(x_ref, unit_ref, m_ref, *outs):
    bins = x_ref.shape[1] // 2
    width = m_ref.shape[1]
    block = 3 * HALF
    unit = unit_ref[0:1, :]
    both = jnp.transpose(x_ref[...], (1, 0, 2))
    norm = jnp.max(jnp.max(x_ref[:, 0, 3 * HALF :], axis=0, keepdims=True))
    for k in range(bins):
        for i in range(3):
            cut = slice(i * HALF, (i + 1) * HALF)
            rows = jnp.concatenate([both[k][:, cut], both[bins + k][:, cut]], axis=1) * unit
            for o_ref in outs:
                o_ref[cut, k, :] = rows
            m_ref[k * block + i * HALF : k * block + (i + 1) * HALF, :] = rows.astype(BF16)
    m_ref[bins * block :, :] = jnp.full((16, width), norm, F32).astype(BF16)


def source_unpack(x, unit, bins, full):
    block, width = 3 * HALF, 2 * HALF
    out = [jax.ShapeDtypeStruct((bins * block + 16, width), BF16)]
    if full:
        out.append(jax.ShapeDtypeStruct((block, bins, width), F32))
    return call(source_unpack_kernel, out, [vmem()] * 2, 0, 16 * bins * block * width)(x, unit)


def plus_kernel(x_ref, init_ref, unit_ref, o_ref):
    bins, _, recs = init_ref.shape
    unit = jnp.max(unit_ref[...])
    both = jnp.transpose(x_ref[...], (1, 0, 2))
    for k in range(bins):
        rows = jnp.concatenate([both[k], both[bins + k]], axis=0) * unit
        o_ref[k] = (init_ref[k].astype(F32) + rows).astype(BF16)


def plus_call(x, init, unit):
    return call(plus_kernel, jax.ShapeDtypeStruct(init.shape, BF16), [vmem()] * 3, 0, 8 * x.size)(x, init, unit)


def final_kernel(x_ref, init_ref, unit_ref, o_ref):
    bins = init_ref.shape[0]
    unit = jnp.max(unit_ref[...])
    both = jnp.transpose(x_ref[...], (1, 0, 2))
    for k in range(bins):
        rows = jnp.concatenate([both[k], both[bins + k]], axis=0) * unit
        o_ref[:, k, :] = (init_ref[k].astype(F32) + rows).T


def final_call(x, init, unit):
    bins, width, recs = init.shape
    out = jax.ShapeDtypeStruct((recs, bins, width), F32)
    return call(final_kernel, out, [vmem()] * 3, 0, 8 * x.size)(x, init, unit)


def body(response, focus_init, onset_src, onset_rec):
    nfreq = lax.axis_size("freq")
    freq_pos = lax.axis_index("freq")
    rec_pos = lax.axis_index("rec")
    _, bins, sources, recs = response.shape
    width = focus_init.shape[2]
    block = sources // 4
    core, high = rec_pos % 2, rec_pos // 2
    tables = [jnp.asarray(t) for t in fold_tables(bins * nfreq)]

    def place(h, c):
        return h * 2 + c

    order = jnp.stack([place(1 - high, 1 - core), place(1 - high, core), place(high, 1 - core), place(high, core)])
    order = order.astype(jnp.int32)

    rec_onsets = lax.dynamic_slice_in_dim(onset_rec.T, freq_pos, 1, 0)
    mine = lax.dynamic_slice(onset_src.reshape(4, 3, HALF, HALF), (rec_pos, 0, freq_pos, 0), (1, 3, 1, HALF))
    src_onsets = jnp.concatenate([mine.reshape(1, 3 * HALF), jnp.zeros((1, HALF), jnp.int32)], axis=1)

    def swap(values):
        return lax.all_to_all(values.astype(F16), "freq", split_axis=0, concat_axis=0, tiled=True).astype(F32)

    def step_to(values, pairs):
        return lax.ppermute(values, "rec", pairs)

    init_norm = math.sqrt(2.0 * bins * nfreq) * INIT_ABS
    rec_gain = 4 * recs * R_ABS

    init_t = jnp.transpose(focus_init, (1, 2, 0))
    init_t, order, src_onsets, rec_onsets = lax.optimization_barrier((init_t, order, src_onsets, rec_onsets))
    plus = init_t
    bound = jnp.full((8, 128), rec_gain * init_norm, F32)
    scale, unit = TOP / bound, bound * (1.0 / TOP)
    minus_out = None
    plus_out = None
    for step in range(ITERS):
        last = step == ITERS - 1
        away = forward_call(order, response, plus, (0, 2))
        away_other = step_to(away, CORE_SWAP)
        away_mine = forward_call(order, response, plus, (1,))
        coded = ((away_mine[0] + away_other[0]) * scale[0, 0]).astype(F16)
        coded, plus = lax.optimization_barrier((coded, plus))
        far = step_to(coded, HIGH_SWAP)
        near = forward_call(order, response, plus, (3,))
        field = source_pack(near, away_other, far.astype(F32), scale)
        field = swap(field)
        field = window_call(field, src_onsets, tables, True)
        mine, *full = source_unpack(swap(field), unit, bins, last)
        if last:
            minus_out = full[0]
        across = step_to(mine, HIGH_SWAP)
        beside = step_to(mine, CORE_SWAP)
        total = adjoint_first(order, response, mine, beside)
        across, total = lax.optimization_barrier((across, total))
        corner = step_to(across, CORE_SWAP)
        parts = (mine, beside, across, corner)
        behind, back_unit, scale, unit = adjoint_last(order, response, total, unit, parts, rec_gain, init_norm)
        field = window_call(swap(behind), rec_onsets, tables, False)
        back = swap(field)
        if last:
            plus_out = final_call(back, init_t, back_unit)
        else:
            plus = plus_call(back, init_t, back_unit)
    return (minus_out, plus_out)


def solution(mesh):
    return jax.shard_map(
        body,
        mesh=mesh,
        in_specs=(P(None, "freq", None, "rec"), P("rec", "freq", None), P(), P("rec", None)),
        out_specs=(P("rec", "freq", None), P("rec", "freq", None)),
        check_vma=False,
    )
```

```python
import math

import jax
import jax.numpy as jnp
import numpy as np
from jax import lax
from jax.experimental import pallas as pl
from jax.experimental.pallas import tpu as pltpu
from jax.sharding import PartitionSpec as P

NT = 640
ITERS = 2
HALF = 64
FOLD = 336
R_ABS = 0.078125 * math.sqrt(2.0) * 1.001
INIT_ABS = 6.0
TOP = 16384.0
FLOOR = 2.0 ** -14
MIB = 1024 * 1024
F32 = jnp.float32
BF16 = jnp.bfloat16
F16 = jnp.float16

CORE_SWAP = [(0, 1), (1, 0), (2, 3), (3, 2)]
HIGH_SWAP = [(0, 2), (2, 0), (1, 3), (3, 1)]


def vmem():
    return pl.BlockSpec(memory_space=pltpu.VMEM)


def smem():
    return pl.BlockSpec(memory_space=pltpu.SMEM)


def call(kernel, out_shape, specs, flops, moved, limit=8):
    return pl.pallas_call(
        kernel,
        in_specs=specs,
        out_specs=jax.tree.map(lambda _: vmem(), out_shape),
        out_shape=out_shape,
        compiler_params=pltpu.CompilerParams(vmem_limit_bytes=limit * MIB),
        cost_estimate=pl.CostEstimate(flops=flops, bytes_accessed=moved, transcendentals=0),
    )


def high_low(values):
    values = np.asarray(values, np.float32)
    high = values.astype(jnp.bfloat16)
    return [high, (values - high.astype(np.float32)).astype(jnp.bfloat16)]


def fold_tables(nbins):
    bins = np.arange(nbins, dtype=np.int64) + 1
    samples = np.arange(FOLD, dtype=np.int64)
    angles = ((bins[:, None] * samples[None, :]) % NT).astype(np.float64) * (2.0 * math.pi / NT)
    used = samples[None, :] <= NT // 2
    cosine = np.where(used, np.cos(angles), 0.0)
    sine = np.where(used, np.sin(angles), 0.0)
    forward = np.stack(high_low(cosine) + high_low(sine))
    inverse = np.stack(high_low(cosine.T * (2.0 / NT)) + high_low(sine.T * (2.0 / NT)))
    return forward, inverse


def split_dot(high, low, x):
    x_high = x.astype(BF16)
    x_low = (x - x_high.astype(F32)).astype(BF16)
    total = jnp.dot(high, x_high, preferred_element_type=F32)
    total = total + jnp.dot(high, x_low, preferred_element_type=F32)
    return total + jnp.dot(low, x_high, preferred_element_type=F32)


def pair_halves(x_ref, first):
    blocks, _, lanes = x_ref.shape
    x = x_ref[...].reshape(blocks // 2, 2, 8, lanes)
    even, odd = x[:, 0], x[:, 1]
    real = jnp.where(first, even, pltpu.roll(odd, 4, 1))
    imag = jnp.where(first, pltpu.roll(even, 4, 1), odd)
    return real.reshape(blocks * 4, lanes), imag.reshape(blocks * 4, lanes)


def triple_halves(x_ref, first):
    groups = x_ref.shape[0] // 24
    x = x_ref[...].reshape(groups, 3, 8, 2 * HALF)
    a, b, c = x[:, 0], x[:, 1], x[:, 2]
    first = first[:, :, : 2 * HALF]
    real = jnp.where(first, a, b).reshape(groups * 8, 2 * HALF)
    imag = pltpu.roll(jnp.where(first, c, a), 4, 1).reshape(groups * 8, 2 * HALF)
    rest = jnp.where(first, b, c).reshape(groups * 8, 2 * HALF)
    return jnp.concatenate([real, rest], axis=1), jnp.concatenate([imag, pltpu.roll(rest, HALF, 1)], axis=1)


def window_kernel(from_source, x_ref, onset_ref, forward_ref, inverse_ref, o_ref):
    blocks, _, lanes = o_ref.shape
    first = lax.broadcasted_iota(jnp.int32, (blocks // 2, 8, lanes), 1) < 4
    real, imag = triple_halves(x_ref, first) if from_source else pair_halves(x_ref, first)
    a = split_dot(inverse_ref[0], inverse_ref[1], real)
    b = split_dot(inverse_ref[2], inverse_ref[3], imag)
    n = lax.broadcasted_iota(jnp.int32, a.shape, 0)
    onset = onset_ref[...]
    near = jnp.where(n < onset, a - b, 0.0)
    far = jnp.where((NT - n < onset) & (n > 0) & (n < NT // 2), a + b, 0.0)
    real = split_dot(forward_ref[0], forward_ref[1], near + far)
    imag = split_dot(forward_ref[2], forward_ref[3], far - near)
    norm = None
    if from_source:
        norm = jnp.sqrt(jnp.max(jnp.sum(real * real + imag * imag, axis=0, keepdims=True))) * 1.01
    real = real.reshape(blocks // 2, 8, lanes)
    imag = imag.reshape(blocks // 2, 8, lanes)
    even = jnp.where(first, real, pltpu.roll(imag, 4, 1))
    odd = jnp.where(first, pltpu.roll(real, 4, 1), imag)
    if from_source:
        spare = lax.broadcasted_iota(jnp.int32, even.shape, 2) >= 3 * HALF
        even = jnp.where(spare, norm, even)
        odd = jnp.where(spare, norm, odd)
    o_ref[...] = jnp.concatenate([even[:, None], odd[:, None]], axis=1).reshape(blocks, 8, lanes)


def window_call(x, onsets, tables, from_source):
    lanes = onsets.shape[1]
    blocks = x.shape[0] // 12 if from_source else x.shape[0]
    return call(
        lambda *refs: window_kernel(from_source, *refs),
        jax.ShapeDtypeStruct((blocks, 8, lanes), F32),
        [vmem()] * 4,
        12 * FOLD * 512 * lanes,
        2 * 4 * x.size,
        16,
    )(x, onsets, *tables)


def forward_bin(picks, order_ref, r_ref, x_ref, o_ref, k):
    block = o_ref.shape[2]
    dims = (((1,), (1,)), ((), ()))
    x = x_ref[k]
    y = jnp.concatenate([-x[HALF:], x[:HALF]], axis=0)
    starts = [pl.multiple_of(order_ref[pick] * block, HALF) for pick in picks]
    real = jnp.concatenate([r_ref[0, k, pl.ds(at, block), :] for at in starts], axis=0)
    imag = jnp.concatenate([r_ref[1, k, pl.ds(at, block), :] for at in starts], axis=0)
    both = lax.dot_general(real, x, dims, preferred_element_type=F32)
    both = both + lax.dot_general(imag, y, dims, preferred_element_type=F32)
    for i in range(len(picks)):
        o_ref[i, k] = both[i * block : (i + 1) * block]


def forward_kernel(picks, order_ref, r_ref, x_ref, o_ref):
    for k in range(o_ref.shape[1]):
        forward_bin(picks, order_ref, r_ref, x_ref, o_ref, k)


def forward_call(order, response, plus, picks):
    _, bins, sources, recs = response.shape
    width = plus.shape[1]
    block = sources // 4
    return call(
        lambda *refs: forward_kernel(picks, *refs),
        jax.ShapeDtypeStruct((len(picks), bins, block, width), F32),
        [smem(), vmem(), vmem()],
        4 * bins * len(picks) * block * recs * width,
        4 * bins * len(picks) * block * recs,
    )(order, response, plus)


def adjoint_sum(order_ref, picks, r_ref, parts, k):
    block = r_ref.shape[2] // 4
    m = jnp.concatenate([part[k * block : (k + 1) * block, :] for part in parts], axis=0).T
    n = jnp.concatenate([m[HALF:], -m[:HALF]], axis=0)
    starts = [pl.multiple_of(order_ref[pick] * block, HALF) for pick in picks]
    real = jnp.concatenate([r_ref[0, k, pl.ds(at, block), :] for at in starts], axis=0)
    imag = jnp.concatenate([r_ref[1, k, pl.ds(at, block), :] for at in starts], axis=0)
    return jnp.dot(m, real, preferred_element_type=F32) + jnp.dot(n, imag, preferred_element_type=F32)


def adjoint_first_kernel(order_ref, r_ref, a_ref, b_ref, o_ref):
    for k in range(r_ref.shape[1]):
        o_ref[k] = adjoint_sum(order_ref, (3, 2), r_ref, (a_ref, b_ref), k)


def adjoint_first(order, response, mine, beside):
    _, bins, sources, recs = response.shape
    width = mine.shape[1]
    return call(
        adjoint_first_kernel,
        jax.ShapeDtypeStruct((bins, width, recs), F32),
        [smem()] + [vmem()] * 3,
        2 * bins * sources * recs * width,
        2 * bins * sources * recs,
    )(order, response, mine, beside)


def adjoint_last_kernel(
    gain,
    rec_gain,
    init_norm,
    order_ref,
    r_ref,
    total_ref,
    unit_ref,
    a_ref,
    b_ref,
    c_ref,
    d_ref,
    o_ref,
    back_ref,
    next_scale_ref,
    next_unit_ref,
):
    bins = r_ref.shape[1]
    block = r_ref.shape[2] // 4
    recs = r_ref.shape[3]
    peak = a_ref[bins * block :, :]
    for part in (b_ref, c_ref, d_ref):
        peak = jnp.maximum(peak, part[bins * block :, :])
    norm = jnp.maximum(jnp.max(peak.astype(F32), axis=0, keepdims=True), FLOOR)
    norm = jnp.broadcast_to(norm * (1.01 * 1.01 * gain), unit_ref.shape) * unit_ref[...]
    back_ref[...] = norm * (1.0 / TOP)
    after = rec_gain * (init_norm + norm)
    next_scale_ref[...] = TOP / after
    next_unit_ref[...] = after * (1.0 / TOP)
    scale = jnp.max(TOP / norm)
    real, imag = [], []
    for k in range(bins):
        both = total_ref[k] + adjoint_sum(order_ref, (1, 0), r_ref, (c_ref, d_ref), k)
        both = both * scale
        real.append(both[:HALF][None])
        imag.append(both[HALF:][None])
    both = jnp.concatenate(real + imag, axis=0)
    o_ref[...] = jnp.transpose(both, (1, 0, 2))


def adjoint_last(order, response, total, unit, parts, rec_gain, init_norm):
    _, bins, sources, recs = response.shape
    width = total.shape[1]
    gain = sources * R_ABS
    stat = jax.ShapeDtypeStruct(unit.shape, F32)
    return call(
        lambda *refs: adjoint_last_kernel(gain, rec_gain, init_norm, *refs),
        (jax.ShapeDtypeStruct((HALF, 2 * bins, recs), F32), stat, stat, stat),
        [smem()] + [vmem()] * 7,
        2 * bins * sources * recs * width,
        2 * bins * sources * recs,
    )(order, response, total, unit, *parts)


def source_pack_kernel(kept_ref, other_ref, far_ref, scale_ref, o_ref):
    _, bins, block, width = kept_ref.shape
    scale = scale_ref[0:1, :]
    for k in range(bins):
        total = (kept_ref[0, k] + other_ref[1, k]) * scale + far_ref[k]
        a, b = total[:HALF], total[HALF : 2 * HALF]
        o_ref[:, 0, k, :] = jnp.concatenate([a[:, :HALF], b[:, :HALF]], axis=1)
        o_ref[:, 1, k, :] = jnp.concatenate([a[:, HALF:], b[:, HALF:]], axis=1)
        o_ref[:, 2, k, :] = total[2 * HALF :]


def source_pack(kept, other, far, scale):
    bins = kept.shape[1]
    return call(
        source_pack_kernel,
        jax.ShapeDtypeStruct((HALF, 3, bins, 2 * HALF), F32),
        [vmem()] * 4,
        0,
        16 * kept.size,
    )(kept, other, far, scale)


def source_unpack_kernel(x_ref, unit_ref, m_ref, *outs):
    bins = x_ref.shape[1] // 2
    width = m_ref.shape[1]
    block = 3 * HALF
    unit = unit_ref[0:1, :]
    both = jnp.transpose(x_ref[...], (1, 0, 2))
    norm = jnp.max(jnp.max(x_ref[:, 0, 3 * HALF :], axis=0, keepdims=True))
    for k in range(bins):
        for i in range(3):
            cut = slice(i * HALF, (i + 1) * HALF)
            rows = jnp.concatenate([both[k][:, cut], both[bins + k][:, cut]], axis=1) * unit
            for o_ref in outs:
                o_ref[cut, k, :] = rows
            m_ref[k * block + i * HALF : k * block + (i + 1) * HALF, :] = rows.astype(BF16)
    m_ref[bins * block :, :] = jnp.full((16, width), norm, F32).astype(BF16)


def source_unpack(x, unit, bins, full):
    block, width = 3 * HALF, 2 * HALF
    out = [jax.ShapeDtypeStruct((bins * block + 16, width), BF16)]
    if full:
        out.append(jax.ShapeDtypeStruct((block, bins, width), F32))
    return call(source_unpack_kernel, out, [vmem()] * 2, 0, 16 * bins * block * width)(x, unit)


def plus_forward_kernel(picks, order_ref, r_ref, back_ref, init_ref, unit_ref, x_ref, o_ref):
    bins, _, recs = init_ref.shape
    unit = jnp.max(unit_ref[...])
    both = jnp.transpose(back_ref[...], (1, 0, 2))
    for k in range(bins):
        rows = jnp.concatenate([both[k], both[bins + k]], axis=0) * unit
        x_ref[k] = (init_ref[k].astype(F32) + rows).astype(BF16)
        forward_bin(picks, order_ref, r_ref, x_ref, o_ref, k)


def plus_forward(order, response, back, init, unit, picks):
    bins, width, recs = init.shape
    block = response.shape[2] // 4
    return call(
        lambda *refs: plus_forward_kernel(picks, *refs),
        [
            jax.ShapeDtypeStruct(init.shape, BF16),
            jax.ShapeDtypeStruct((len(picks), bins, block, width), F32),
        ],
        [smem()] + [vmem()] * 4,
        4 * bins * len(picks) * block * recs * width,
        4 * bins * len(picks) * block * recs,
    )(order, response, back, init, unit)


def final_kernel(x_ref, init_ref, unit_ref, o_ref):
    bins = init_ref.shape[0]
    unit = jnp.max(unit_ref[...])
    both = jnp.transpose(x_ref[...], (1, 0, 2))
    for k in range(bins):
        rows = jnp.concatenate([both[k], both[bins + k]], axis=0) * unit
        o_ref[:, k, :] = (init_ref[k].astype(F32) + rows).T


def final_call(x, init, unit):
    bins, width, recs = init.shape
    out = jax.ShapeDtypeStruct((recs, bins, width), F32)
    return call(final_kernel, out, [vmem()] * 3, 0, 8 * x.size)(x, init, unit)


def body(response, focus_init, onset_src, onset_rec):
    nfreq = lax.axis_size("freq")
    freq_pos = lax.axis_index("freq")
    rec_pos = lax.axis_index("rec")
    _, bins, sources, recs = response.shape
    width = focus_init.shape[2]
    block = sources // 4
    core, high = rec_pos % 2, rec_pos // 2
    tables = [jnp.asarray(t) for t in fold_tables(bins * nfreq)]

    def place(h, c):
        return h * 2 + c

    order = jnp.stack([place(1 - high, 1 - core), place(1 - high, core), place(high, 1 - core), place(high, core)])
    order = order.astype(jnp.int32)

    rec_onsets = lax.dynamic_slice_in_dim(onset_rec.T, freq_pos, 1, 0)
    mine = lax.dynamic_slice(onset_src.reshape(4, 3, HALF, HALF), (rec_pos, 0, freq_pos, 0), (1, 3, 1, HALF))
    src_onsets = jnp.concatenate([mine.reshape(1, 3 * HALF), jnp.zeros((1, HALF), jnp.int32)], axis=1)

    def swap(values):
        return lax.all_to_all(values.astype(F16), "freq", split_axis=0, concat_axis=0, tiled=True).astype(F32)

    def step_to(values, pairs):
        return lax.ppermute(values, "rec", pairs)

    init_norm = math.sqrt(2.0 * bins * nfreq) * INIT_ABS
    rec_gain = 4 * recs * R_ABS

    init_t = jnp.transpose(focus_init, (1, 2, 0))
    init_t, order, src_onsets, rec_onsets = lax.optimization_barrier((init_t, order, src_onsets, rec_onsets))
    plus = init_t
    bound = jnp.full((1, 128), rec_gain * init_norm, F32)
    scale, unit = TOP / bound, bound * (1.0 / TOP)
    minus_out = None
    plus_out = None
    for step in range(ITERS):
        last = step == ITERS - 1
        if step == 0:
            away = forward_call(order, response, plus, (0, 2))
        else:
            plus, away = plus_forward(order, response, back, init_t, back_unit, (0, 2))
        away_other = step_to(away, CORE_SWAP)
        away_mine = forward_call(order, response, plus, (1,))
        coded = ((away_mine[0] + away_other[0]) * scale).astype(F16)
        coded, plus = lax.optimization_barrier((coded, plus))
        far = step_to(coded, HIGH_SWAP)
        near = forward_call(order, response, plus, (3,))
        field = source_pack(near, away_other, far.astype(F32), scale)
        field = swap(field).reshape(3 * HALF * bins, width)
        field = window_call(field, src_onsets, tables, True)
        mine, *full = source_unpack(swap(field), unit, bins, last)
        if last:
            minus_out = full[0]
        across = step_to(mine, HIGH_SWAP)
        beside = step_to(mine, CORE_SWAP)
        total = adjoint_first(order, response, mine, beside)
        across, total = lax.optimization_barrier((across, total))
        corner = step_to(across, CORE_SWAP)
        parts = (mine, beside, across, corner)
        behind, back_unit, scale, unit = adjoint_last(order, response, total, unit, parts, rec_gain, init_norm)
        field = window_call(swap(behind), rec_onsets, tables, False)
        back = swap(field)
        if last:
            plus_out = final_call(back, init_t, back_unit)
    return (minus_out, plus_out)


def solution(mesh):
    return jax.shard_map(
        body,
        mesh=mesh,
        in_specs=(P(None, "freq", None, "rec"), P("rec", "freq", None), P(), P("rec", None)),
        out_specs=(P("rec", "freq", None), P("rec", "freq", None)),
        check_vma=False,
    )
```

```python
import math

import jax
import jax.numpy as jnp
import numpy as np
from jax import lax
from jax.experimental import pallas as pl
from jax.experimental.pallas import tpu as pltpu
from jax.sharding import PartitionSpec as P

NT = 640
ITERS = 2
HALF = 64
FOLD = 336
R_ABS = 0.078125 * math.sqrt(2.0) * 1.001
INIT_ABS = 6.0
TOP = 16384.0
FLOOR = 2.0 ** -14
MIB = 1024 * 1024
F32 = jnp.float32
BF16 = jnp.bfloat16
F16 = jnp.float16

CORE_SWAP = [(0, 1), (1, 0), (2, 3), (3, 2)]
HIGH_SWAP = [(0, 2), (2, 0), (1, 3), (3, 1)]


def vmem():
    return pl.BlockSpec(memory_space=pltpu.VMEM)


def smem():
    return pl.BlockSpec(memory_space=pltpu.SMEM)


def call(kernel, out_shape, specs, flops, moved, limit=8):
    return pl.pallas_call(
        kernel,
        in_specs=specs,
        out_specs=jax.tree.map(lambda _: vmem(), out_shape),
        out_shape=out_shape,
        compiler_params=pltpu.CompilerParams(vmem_limit_bytes=limit * MIB),
        cost_estimate=pl.CostEstimate(flops=flops, bytes_accessed=moved, transcendentals=0),
    )


def high_low(values):
    values = np.asarray(values, np.float32)
    high = values.astype(jnp.bfloat16)
    return [high, (values - high.astype(np.float32)).astype(jnp.bfloat16)]


def fold_tables(nbins):
    bins = np.arange(nbins, dtype=np.int64) + 1
    samples = np.arange(FOLD, dtype=np.int64)
    angles = ((bins[:, None] * samples[None, :]) % NT).astype(np.float64) * (2.0 * math.pi / NT)
    used = samples[None, :] <= NT // 2
    cosine = np.where(used, np.cos(angles), 0.0)
    sine = np.where(used, np.sin(angles), 0.0)
    forward = np.stack(high_low(cosine) + high_low(sine))
    inverse = np.stack(high_low(cosine.T * (2.0 / NT)) + high_low(sine.T * (2.0 / NT)))
    return forward, inverse


def split_dot(high, low, x):
    x_high = x.astype(BF16)
    x_low = (x - x_high.astype(F32)).astype(BF16)
    total = jnp.dot(high, x_high, preferred_element_type=F32)
    total = total + jnp.dot(high, x_low, preferred_element_type=F32)
    return total + jnp.dot(low, x_high, preferred_element_type=F32)


def pair_halves(x_ref, first):
    blocks, _, lanes = x_ref.shape
    x = x_ref[...].reshape(blocks // 2, 2, 8, lanes)
    even, odd = x[:, 0], x[:, 1]
    real = jnp.where(first, even, pltpu.roll(odd, 4, 1))
    imag = jnp.where(first, pltpu.roll(even, 4, 1), odd)
    return real.reshape(blocks * 4, lanes), imag.reshape(blocks * 4, lanes)


def triple_halves(x_ref, first):
    groups = x_ref.shape[0] // 24
    x = x_ref[...].reshape(groups, 3, 8, 2 * HALF)
    a, b, c = x[:, 0], x[:, 1], x[:, 2]
    first = first[:, :, : 2 * HALF]
    real = jnp.where(first, a, b).reshape(groups * 8, 2 * HALF)
    imag = pltpu.roll(jnp.where(first, c, a), 4, 1).reshape(groups * 8, 2 * HALF)
    rest = jnp.where(first, b, c).reshape(groups * 8, 2 * HALF)
    return jnp.concatenate([real, rest], axis=1), jnp.concatenate([imag, pltpu.roll(rest, HALF, 1)], axis=1)


def window_kernel(from_source, x_ref, onset_ref, forward_ref, inverse_ref, o_ref):
    blocks, _, lanes = o_ref.shape
    first = lax.broadcasted_iota(jnp.int32, (blocks // 2, 8, lanes), 1) < 4
    real, imag = triple_halves(x_ref, first) if from_source else pair_halves(x_ref, first)
    a = split_dot(inverse_ref[0], inverse_ref[1], real)
    b = split_dot(inverse_ref[2], inverse_ref[3], imag)
    n = lax.broadcasted_iota(jnp.int32, a.shape, 0)
    onset = onset_ref[...]
    near = jnp.where(n < onset, a - b, 0.0)
    far = jnp.where((NT - n < onset) & (n > 0) & (n < NT // 2), a + b, 0.0)
    real = split_dot(forward_ref[0], forward_ref[1], near + far)
    imag = split_dot(forward_ref[2], forward_ref[3], far - near)
    norm = None
    if from_source:
        norm = jnp.sqrt(jnp.max(jnp.sum(real * real + imag * imag, axis=0, keepdims=True))) * 1.01
    real = real.reshape(blocks // 2, 8, lanes)
    imag = imag.reshape(blocks // 2, 8, lanes)
    even = jnp.where(first, real, pltpu.roll(imag, 4, 1))
    odd = jnp.where(first, pltpu.roll(real, 4, 1), imag)
    if from_source:
        spare = lax.broadcasted_iota(jnp.int32, even.shape, 2) >= 3 * HALF
        even = jnp.where(spare, norm, even)
        odd = jnp.where(spare, norm, odd)
    o_ref[...] = jnp.concatenate([even[:, None], odd[:, None]], axis=1).reshape(blocks, 8, lanes)


def window_call(x, onsets, tables, from_source):
    lanes = onsets.shape[1]
    blocks = x.shape[0] // 12 if from_source else x.shape[0]
    return call(
        lambda *refs: window_kernel(from_source, *refs),
        jax.ShapeDtypeStruct((blocks, 8, lanes), F32),
        [vmem()] * 4,
        12 * FOLD * 512 * lanes,
        2 * 4 * x.size,
        16,
    )(x, onsets, *tables)


def forward_bin(picks, order_ref, r_ref, x_ref, o_ref, k):
    block = o_ref.shape[2]
    dims = (((1,), (1,)), ((), ()))
    x = x_ref[k]
    y = jnp.concatenate([-x[HALF:], x[:HALF]], axis=0)
    starts = [pl.multiple_of(order_ref[pick] * block, HALF) for pick in picks]
    real = jnp.concatenate([r_ref[0, k, pl.ds(at, block), :] for at in starts], axis=0)
    imag = jnp.concatenate([r_ref[1, k, pl.ds(at, block), :] for at in starts], axis=0)
    both = lax.dot_general(real, x, dims, preferred_element_type=F32)
    both = both + lax.dot_general(imag, y, dims, preferred_element_type=F32)
    for i in range(len(picks)):
        o_ref[i, k] = both[i * block : (i + 1) * block]


def forward_kernel(picks, order_ref, r_ref, x_ref, o_ref):
    for k in range(o_ref.shape[1]):
        forward_bin(picks, order_ref, r_ref, x_ref, o_ref, k)


def forward_call(order, response, plus, picks):
    _, bins, sources, recs = response.shape
    width = plus.shape[1]
    block = sources // 4
    return call(
        lambda *refs: forward_kernel(picks, *refs),
        jax.ShapeDtypeStruct((len(picks), bins, block, width), F32),
        [smem(), vmem(), vmem()],
        4 * bins * len(picks) * block * recs * width,
        4 * bins * len(picks) * block * recs,
    )(order, response, plus)


def adjoint_sum(order_ref, picks, r_ref, parts, k):
    block = r_ref.shape[2] // 4
    m = jnp.concatenate([part[k * block : (k + 1) * block, :] for part in parts], axis=0).T
    n = jnp.concatenate([m[HALF:], -m[:HALF]], axis=0)
    starts = [pl.multiple_of(order_ref[pick] * block, HALF) for pick in picks]
    real = jnp.concatenate([r_ref[0, k, pl.ds(at, block), :] for at in starts], axis=0)
    imag = jnp.concatenate([r_ref[1, k, pl.ds(at, block), :] for at in starts], axis=0)
    return jnp.dot(m, real, preferred_element_type=F32) + jnp.dot(n, imag, preferred_element_type=F32)


def adjoint_first_kernel(order_ref, r_ref, a_ref, b_ref, o_ref):
    for k in range(r_ref.shape[1]):
        o_ref[k] = adjoint_sum(order_ref, (3, 2), r_ref, (a_ref, b_ref), k)


def adjoint_first(order, response, mine, beside):
    _, bins, sources, recs = response.shape
    width = mine.shape[1]
    return call(
        adjoint_first_kernel,
        jax.ShapeDtypeStruct((bins, width, recs), F32),
        [smem()] + [vmem()] * 3,
        2 * bins * sources * recs * width,
        2 * bins * sources * recs,
    )(order, response, mine, beside)


def adjoint_middle_kernel(order_ref, r_ref, total_ref, part_ref, o_ref):
    for k in range(r_ref.shape[1]):
        o_ref[k] = total_ref[k] + adjoint_sum(order_ref, (1,), r_ref, (part_ref,), k)


def adjoint_middle(order, response, total, part):
    _, bins, sources, recs = response.shape
    return call(
        adjoint_middle_kernel,
        jax.ShapeDtypeStruct(total.shape, F32),
        [smem()] + [vmem()] * 3,
        bins * sources * recs * total.shape[1],
        bins * sources * recs,
    )(order, response, total, part)


def adjoint_last_kernel(
    gain,
    rec_gain,
    init_norm,
    order_ref,
    r_ref,
    total_ref,
    unit_ref,
    a_ref,
    b_ref,
    c_ref,
    d_ref,
    o_ref,
    back_ref,
    next_scale_ref,
    next_unit_ref,
):
    bins = r_ref.shape[1]
    block = r_ref.shape[2] // 4
    recs = r_ref.shape[3]
    peak = a_ref[bins * block :, :]
    for part in (b_ref, c_ref, d_ref):
        peak = jnp.maximum(peak, part[bins * block :, :])
    norm = jnp.maximum(jnp.max(peak.astype(F32), axis=0, keepdims=True), FLOOR)
    norm = jnp.broadcast_to(norm * (1.01 * 1.01 * gain), unit_ref.shape) * unit_ref[...]
    back_ref[...] = norm * (1.0 / TOP)
    after = rec_gain * (init_norm + norm)
    next_scale_ref[...] = TOP / after
    next_unit_ref[...] = after * (1.0 / TOP)
    scale = jnp.max(TOP / norm)
    real, imag = [], []
    for k in range(bins):
        both = total_ref[k] + adjoint_sum(order_ref, (0,), r_ref, (d_ref,), k)
        both = both * scale
        real.append(both[:HALF][None])
        imag.append(both[HALF:][None])
    both = jnp.concatenate(real + imag, axis=0)
    o_ref[...] = jnp.transpose(both, (1, 0, 2))


def adjoint_last(order, response, total, unit, parts, rec_gain, init_norm):
    _, bins, sources, recs = response.shape
    width = total.shape[1]
    gain = sources * R_ABS
    stat = jax.ShapeDtypeStruct(unit.shape, F32)
    return call(
        lambda *refs: adjoint_last_kernel(gain, rec_gain, init_norm, *refs),
        (jax.ShapeDtypeStruct((HALF, 2 * bins, recs), F32), stat, stat, stat),
        [smem()] + [vmem()] * 7,
        2 * bins * sources * recs * width,
        2 * bins * sources * recs,
    )(order, response, total, unit, *parts)


def source_pack_kernel(kept_ref, other_ref, far_ref, scale_ref, o_ref):
    _, bins, block, width = kept_ref.shape
    scale = scale_ref[0:1, :]
    for k in range(bins):
        total = (kept_ref[0, k] + other_ref[1, k]) * scale + far_ref[k]
        a, b = total[:HALF], total[HALF : 2 * HALF]
        o_ref[:, 0, k, :] = jnp.concatenate([a[:, :HALF], b[:, :HALF]], axis=1)
        o_ref[:, 1, k, :] = jnp.concatenate([a[:, HALF:], b[:, HALF:]], axis=1)
        o_ref[:, 2, k, :] = total[2 * HALF :]


def source_pack(kept, other, far, scale):
    bins = kept.shape[1]
    return call(
        source_pack_kernel,
        jax.ShapeDtypeStruct((HALF, 3, bins, 2 * HALF), F32),
        [vmem()] * 4,
        0,
        16 * kept.size,
    )(kept, other, far, scale)


def source_rows(both, bins, k, i, unit):
    cut = slice(i * HALF, (i + 1) * HALF)
    return jnp.concatenate([both[k][:, cut], both[bins + k][:, cut]], axis=1) * unit


def source_unpack_kernel(x_ref, unit_ref, m_ref):
    bins, width = x_ref.shape[1] // 2, m_ref.shape[1]
    unit = unit_ref[0:1, :]
    both = jnp.transpose(x_ref[...], (1, 0, 2))
    norm = jnp.max(jnp.max(x_ref[:, 0, 3 * HALF :], axis=0, keepdims=True))
    at = 0
    for k in range(bins):
        for i in range(3):
            m_ref[at : at + HALF, :] = source_rows(both, bins, k, i, unit).astype(BF16)
            at += HALF
    m_ref[at:, :] = jnp.full((16, width), norm, F32).astype(BF16)


def source_unpack(x, unit):
    out = jax.ShapeDtypeStruct((x.shape[1] // 2 * 3 * HALF + 16, 2 * HALF), BF16)
    return call(source_unpack_kernel, out, [vmem()] * 2, 0, 6 * x.size)(x, unit)


def source_output_kernel(x_ref, unit_ref, o_ref):
    bins = x_ref.shape[1] // 2
    unit = unit_ref[0:1, :]
    both = jnp.transpose(x_ref[...], (1, 0, 2))
    for k in range(bins):
        for i in range(3):
            o_ref[i * HALF : (i + 1) * HALF, k, :] = source_rows(both, bins, k, i, unit)


def source_output(x, unit):
    out = jax.ShapeDtypeStruct((3 * HALF, x.shape[1] // 2, 2 * HALF), F32)
    return call(source_output_kernel, out, [vmem(), vmem()], 0, 8 * x.size)(x, unit)


def onset_kernel(order_ref, src_ref, rec_ref, src_row_ref, rec_row_ref):
    freq, first = order_ref[4], order_ref[5]
    lane = lax.broadcasted_iota(jnp.int32, src_ref.shape, 1)
    src = src_ref[...].astype(F32)
    rows = []
    for i in range(3):
        picked = jnp.where(lane == first + i * HALF + freq, src, 0.0)
        picked = jnp.sum(picked, axis=1, keepdims=True)
        rows.append(jnp.broadcast_to(picked, (HALF, 2 * HALF)).T[0:1, :])
    rows.append(jnp.zeros_like(rows[0]))
    src_row_ref[...] = jnp.concatenate(rows, axis=1).astype(jnp.int32)
    rec_row_ref[...] = rec_ref[pl.ds(freq, 1), :]


def onset_rows(order, src, rec):
    out = [jax.ShapeDtypeStruct((1, 4 * HALF), jnp.int32), jax.ShapeDtypeStruct((1, rec.shape[1]), jnp.int32)]
    return call(onset_kernel, out, [smem(), vmem(), vmem()], 0, 4 * (src.size + rec.size))(order, src, rec)


def plus_forward_kernel(picks, order_ref, r_ref, back_ref, init_ref, unit_ref, x_ref, o_ref):
    bins, _, recs = init_ref.shape
    unit = jnp.max(unit_ref[...])
    both = jnp.transpose(back_ref[...], (1, 0, 2))
    for k in range(bins):
        rows = jnp.concatenate([both[k], both[bins + k]], axis=0) * unit
        x_ref[k] = (init_ref[k].astype(F32) + rows).astype(BF16)
        forward_bin(picks, order_ref, r_ref, x_ref, o_ref, k)


def plus_forward(order, response, back, init, unit, picks):
    bins, width, recs = init.shape
    block = response.shape[2] // 4
    return call(
        lambda *refs: plus_forward_kernel(picks, *refs),
        [
            jax.ShapeDtypeStruct(init.shape, BF16),
            jax.ShapeDtypeStruct((len(picks), bins, block, width), F32),
        ],
        [smem()] + [vmem()] * 4,
        4 * bins * len(picks) * block * recs * width,
        4 * bins * len(picks) * block * recs,
    )(order, response, back, init, unit)


def final_kernel(x_ref, init_ref, unit_ref, o_ref):
    bins = init_ref.shape[0]
    unit = jnp.max(unit_ref[...])
    both = jnp.transpose(x_ref[...], (1, 0, 2))
    for k in range(bins):
        rows = jnp.concatenate([both[k], both[bins + k]], axis=0) * unit
        o_ref[:, k, :] = (init_ref[k].astype(F32) + rows).T


def final_call(x, init, unit):
    bins, width, recs = init.shape
    out = jax.ShapeDtypeStruct((recs, bins, width), F32)
    return call(final_kernel, out, [vmem()] * 3, 0, 8 * x.size)(x, init, unit)


def body(response, focus_init, onset_src, onset_rec):
    nfreq = lax.axis_size("freq")
    freq_pos = lax.axis_index("freq")
    rec_pos = lax.axis_index("rec")
    _, bins, sources, recs = response.shape
    width = focus_init.shape[2]
    block = sources // 4
    core, high = rec_pos % 2, rec_pos // 2
    tables = [jnp.asarray(t) for t in fold_tables(bins * nfreq)]

    def place(h, c):
        return h * 2 + c

    order = jnp.stack(
        [
            place(1 - high, 1 - core),
            place(1 - high, core),
            place(high, 1 - core),
            place(high, core),
            freq_pos,
            rec_pos * block,
        ]
    ).astype(jnp.int32)

    def swap(values):
        return lax.all_to_all(values.astype(F16), "freq", split_axis=0, concat_axis=0, tiled=True).astype(F32)

    def step_to(values, pairs):
        return lax.ppermute(values, "rec", pairs)

    init_norm = math.sqrt(2.0 * bins * nfreq) * INIT_ABS
    rec_gain = 4 * recs * R_ABS

    init_t = jnp.transpose(focus_init, (1, 2, 0))
    init_t, order = lax.optimization_barrier((init_t, order))
    src_onsets = rec_onsets = None
    plus = init_t
    bound = jnp.full((1, 128), rec_gain * init_norm, F32)
    scale, unit = TOP / bound, bound * (1.0 / TOP)
    minus_out = None
    plus_out = None
    for step in range(ITERS):
        last = step == ITERS - 1
        if step == 0:
            away = forward_call(order, response, plus, (0, 2))
        else:
            plus, away = plus_forward(order, response, back, init_t, back_unit, (0, 2))
        away_other = step_to(away, CORE_SWAP)
        away_mine = forward_call(order, response, plus, (1,))
        coded = ((away_mine[0] + away_other[0]) * scale).astype(F16)
        coded, plus, late = lax.optimization_barrier((coded, plus, order))
        far = step_to(coded, HIGH_SWAP)
        near = forward_call(order, response, plus, (3,))
        if step == 0:
            src_onsets, rec_onsets = onset_rows(late, onset_src.T, onset_rec.T)
        far, src_onsets, rec_onsets = lax.optimization_barrier((far, src_onsets, rec_onsets))
        field = source_pack(near, away_other, far.astype(F32), scale)
        field = swap(field).reshape(3 * HALF * bins, width)
        field = window_call(field, src_onsets, tables, True)
        field = swap(field)
        mine = source_unpack(field, unit)
        across = step_to(mine, HIGH_SWAP)
        beside = step_to(mine, CORE_SWAP)
        total = adjoint_first(order, response, mine, beside)
        if last:
            minus_out = source_output(field, unit)
            across, total, minus_out = lax.optimization_barrier((across, total, minus_out))
        else:
            across, total = lax.optimization_barrier((across, total))
        corner = step_to(across, CORE_SWAP)
        total = adjoint_middle(order, response, total, across)
        parts = (mine, beside, across, corner)
        behind, back_unit, scale, unit = adjoint_last(order, response, total, unit, parts, rec_gain, init_norm)
        field = window_call(swap(behind), rec_onsets, tables, False)
        back = swap(field)
        if last:
            plus_out = final_call(back, init_t, back_unit)
    return (minus_out, plus_out)


def solution(mesh):
    return jax.shard_map(
        body,
        mesh=mesh,
        in_specs=(P(None, "freq", None, "rec"), P("rec", "freq", None), P(), P("rec", None)),
        out_specs=(P("rec", "freq", None), P("rec", "freq", None)),
        check_vma=False,
    )
```

```python
import math

import jax
import jax.numpy as jnp
import numpy as np
from jax import lax
from jax.experimental import pallas as pl
from jax.experimental.pallas import tpu as pltpu
from jax.sharding import PartitionSpec as P

NT = 640
ITERS = 2
HALF = 64
FOLD = 336
R_ABS = 0.078125 * math.sqrt(2.0) * 1.001
INIT_ABS = 6.0
TOP = 16384.0
FLOOR = 2.0 ** -14
MIB = 1024 * 1024
F32 = jnp.float32
BF16 = jnp.bfloat16
F16 = jnp.float16

CORE_SWAP = [(0, 1), (1, 0), (2, 3), (3, 2)]
HIGH_SWAP = [(0, 2), (2, 0), (1, 3), (3, 1)]


def vmem():
    return pl.BlockSpec(memory_space=pltpu.VMEM)


def smem():
    return pl.BlockSpec(memory_space=pltpu.SMEM)


def call(kernel, out_shape, specs, flops, moved, limit=8):
    return pl.pallas_call(
        kernel,
        in_specs=specs,
        out_specs=jax.tree.map(lambda _: vmem(), out_shape),
        out_shape=out_shape,
        compiler_params=pltpu.CompilerParams(vmem_limit_bytes=limit * MIB),
        cost_estimate=pl.CostEstimate(flops=flops, bytes_accessed=moved, transcendentals=0),
    )


def high_low(values):
    values = np.asarray(values, np.float32)
    high = values.astype(jnp.bfloat16)
    return [high, (values - high.astype(np.float32)).astype(jnp.bfloat16)]


def fold_tables(nbins):
    bins = np.arange(nbins, dtype=np.int64) + 1
    samples = np.arange(FOLD, dtype=np.int64)
    angles = ((bins[:, None] * samples[None, :]) % NT).astype(np.float64) * (2.0 * math.pi / NT)
    used = samples[None, :] <= NT // 2
    cosine = np.where(used, np.cos(angles), 0.0)
    sine = np.where(used, np.sin(angles), 0.0)
    forward = np.stack(high_low(cosine) + high_low(sine))
    inverse = np.stack(high_low(cosine.T * (2.0 / NT)) + high_low(sine.T * (2.0 / NT)))
    return forward, inverse


def split_dot(high, low, x):
    x_high = x.astype(BF16)
    x_low = (x - x_high.astype(F32)).astype(BF16)
    total = jnp.dot(high, x_high, preferred_element_type=F32)
    total = total + jnp.dot(high, x_low, preferred_element_type=F32)
    return total + jnp.dot(low, x_high, preferred_element_type=F32)


def pair_halves(x_ref, first):
    blocks, _, lanes = x_ref.shape
    x = x_ref[...].reshape(blocks // 2, 2, 8, lanes)
    even, odd = x[:, 0], x[:, 1]
    real = jnp.where(first, even, pltpu.roll(odd, 4, 1))
    imag = jnp.where(first, pltpu.roll(even, 4, 1), odd)
    return real.reshape(blocks * 4, lanes), imag.reshape(blocks * 4, lanes)


def triple_halves(x_ref, first):
    groups = x_ref.shape[0] // 24
    x = x_ref[...].reshape(groups, 3, 8, 2 * HALF)
    a, b, c = x[:, 0], x[:, 1], x[:, 2]
    first = first[:, :, : 2 * HALF]
    real = jnp.where(first, a, b).reshape(groups * 8, 2 * HALF)
    imag = pltpu.roll(jnp.where(first, c, a), 4, 1).reshape(groups * 8, 2 * HALF)
    rest = jnp.where(first, b, c).reshape(groups * 8, 2 * HALF)
    return jnp.concatenate([real, rest], axis=1), jnp.concatenate([imag, pltpu.roll(rest, HALF, 1)], axis=1)


def window_kernel(from_source, x_ref, onset_ref, forward_ref, inverse_ref, o_ref):
    blocks, _, lanes = o_ref.shape
    first = lax.broadcasted_iota(jnp.int32, (blocks // 2, 8, lanes), 1) < 4
    real, imag = triple_halves(x_ref, first) if from_source else pair_halves(x_ref, first)
    a = split_dot(inverse_ref[0], inverse_ref[1], real)
    b = split_dot(inverse_ref[2], inverse_ref[3], imag)
    n = lax.broadcasted_iota(jnp.int32, a.shape, 0)
    onset = onset_ref[...]
    near = jnp.where(n < onset, a - b, 0.0)
    far = jnp.where((NT - n < onset) & (n > 0) & (n < NT // 2), a + b, 0.0)
    real = split_dot(forward_ref[0], forward_ref[1], near + far)
    imag = split_dot(forward_ref[2], forward_ref[3], far - near)
    norm = None
    if from_source:
        norm = jnp.sqrt(jnp.max(jnp.sum(real * real + imag * imag, axis=0, keepdims=True))) * 1.01
    real = real.reshape(blocks // 2, 8, lanes)
    imag = imag.reshape(blocks // 2, 8, lanes)
    even = jnp.where(first, real, pltpu.roll(imag, 4, 1))
    odd = jnp.where(first, pltpu.roll(real, 4, 1), imag)
    if from_source:
        spare = lax.broadcasted_iota(jnp.int32, even.shape, 2) >= 3 * HALF
        even = jnp.where(spare, norm, even)
        odd = jnp.where(spare, norm, odd)
    o_ref[...] = jnp.concatenate([even[:, None], odd[:, None]], axis=1).reshape(blocks, 8, lanes)


def window_call(x, onsets, tables, from_source):
    lanes = onsets.shape[1]
    blocks = x.shape[0] // 12 if from_source else x.shape[0]
    return call(
        lambda *refs: window_kernel(from_source, *refs),
        jax.ShapeDtypeStruct((blocks, 8, lanes), F32),
        [vmem()] * 4,
        12 * FOLD * 512 * lanes,
        2 * 4 * x.size,
        16,
    )(x, onsets, *tables)


def forward_bin(picks, order_ref, r_ref, x_ref, outs, k):
    block = outs[0].shape[1]
    dims = (((1,), (1,)), ((), ()))
    x = x_ref[k]
    y = jnp.concatenate([-x[HALF:], x[:HALF]], axis=0)
    starts = [pl.multiple_of(order_ref[pick] * block, HALF) for pick in picks]
    real = jnp.concatenate([r_ref[0, k, pl.ds(at, block), :] for at in starts], axis=0)
    imag = jnp.concatenate([r_ref[1, k, pl.ds(at, block), :] for at in starts], axis=0)
    both = lax.dot_general(real, x, dims, preferred_element_type=F32)
    both = both + lax.dot_general(imag, y, dims, preferred_element_type=F32)
    for i, o_ref in enumerate(outs):
        o_ref[k] = both[i * block : (i + 1) * block]


def forward_kernel(picks, order_ref, r_ref, x_ref, *outs):
    for k in range(x_ref.shape[0]):
        forward_bin(picks, order_ref, r_ref, x_ref, outs, k)


def forward_call(order, response, plus, picks):
    _, bins, sources, recs = response.shape
    width = plus.shape[1]
    block = sources // 4
    return call(
        lambda *refs: forward_kernel(picks, *refs),
        [jax.ShapeDtypeStruct((bins, block, width), F32)] * len(picks),
        [smem(), vmem(), vmem()],
        4 * bins * len(picks) * block * recs * width,
        4 * bins * len(picks) * block * recs,
    )(order, response, plus)


def adjoint_sum(order_ref, picks, r_ref, parts, k):
    block = r_ref.shape[2] // 4
    m = jnp.concatenate([part[k * block : (k + 1) * block, :] for part in parts], axis=0).T
    n = jnp.concatenate([m[HALF:], -m[:HALF]], axis=0)
    starts = [pl.multiple_of(order_ref[pick] * block, HALF) for pick in picks]
    real = jnp.concatenate([r_ref[0, k, pl.ds(at, block), :] for at in starts], axis=0)
    imag = jnp.concatenate([r_ref[1, k, pl.ds(at, block), :] for at in starts], axis=0)
    return jnp.dot(m, real, preferred_element_type=F32) + jnp.dot(n, imag, preferred_element_type=F32)


def adjoint_first_kernel(order_ref, r_ref, a_ref, b_ref, o_ref):
    for k in range(r_ref.shape[1]):
        o_ref[k] = adjoint_sum(order_ref, (3, 2), r_ref, (a_ref, b_ref), k)


def adjoint_first(order, response, mine, beside):
    _, bins, sources, recs = response.shape
    width = mine.shape[1]
    return call(
        adjoint_first_kernel,
        jax.ShapeDtypeStruct((bins, width, recs), F32),
        [smem()] + [vmem()] * 3,
        2 * bins * sources * recs * width,
        2 * bins * sources * recs,
    )(order, response, mine, beside)


def adjoint_middle_kernel(order_ref, r_ref, total_ref, part_ref, o_ref):
    for k in range(r_ref.shape[1]):
        o_ref[k] = total_ref[k] + adjoint_sum(order_ref, (1,), r_ref, (part_ref,), k)


def adjoint_middle(order, response, total, part):
    _, bins, sources, recs = response.shape
    return call(
        adjoint_middle_kernel,
        jax.ShapeDtypeStruct(total.shape, F32),
        [smem()] + [vmem()] * 3,
        bins * sources * recs * total.shape[1],
        bins * sources * recs,
    )(order, response, total, part)


def adjoint_last_kernel(
    gain,
    rec_gain,
    init_norm,
    order_ref,
    r_ref,
    total_ref,
    unit_ref,
    a_ref,
    b_ref,
    c_ref,
    d_ref,
    o_ref,
    back_ref,
    next_scale_ref,
    next_unit_ref,
):
    bins = r_ref.shape[1]
    block = r_ref.shape[2] // 4
    recs = r_ref.shape[3]
    peak = a_ref[bins * block :, :]
    for part in (b_ref, c_ref, d_ref):
        peak = jnp.maximum(peak, part[bins * block :, :])
    norm = jnp.maximum(jnp.max(peak.astype(F32), axis=0, keepdims=True), FLOOR)
    norm = jnp.broadcast_to(norm * (1.01 * 1.01 * gain), unit_ref.shape) * unit_ref[...]
    back_ref[...] = norm * (1.0 / TOP)
    after = rec_gain * (init_norm + norm)
    next_scale_ref[...] = TOP / after
    next_unit_ref[...] = after * (1.0 / TOP)
    scale = jnp.max(TOP / norm)
    real, imag = [], []
    for k in range(bins):
        both = total_ref[k] + adjoint_sum(order_ref, (0,), r_ref, (d_ref,), k)
        both = both * scale
        real.append(both[:HALF][None])
        imag.append(both[HALF:][None])
    both = jnp.concatenate(real + imag, axis=0)
    o_ref[...] = jnp.transpose(both, (1, 0, 2))


def adjoint_last(order, response, total, unit, parts, rec_gain, init_norm):
    _, bins, sources, recs = response.shape
    width = total.shape[1]
    gain = sources * R_ABS
    stat = jax.ShapeDtypeStruct(unit.shape, F32)
    return call(
        lambda *refs: adjoint_last_kernel(gain, rec_gain, init_norm, *refs),
        (jax.ShapeDtypeStruct((HALF, 2 * bins, recs), F32), stat, stat, stat),
        [smem()] + [vmem()] * 7,
        2 * bins * sources * recs * width,
        2 * bins * sources * recs,
    )(order, response, total, unit, *parts)


def source_pack_kernel(kept_ref, far_ref, scale_ref, *refs):
    others, o_ref = refs[:-1], refs[-1]
    bins = kept_ref.shape[0]
    scale = scale_ref[0:1, :]
    for k in range(bins):
        total = (kept_ref[k] + (others[0][k] if len(others) == 1 else others[k][...])) * scale + far_ref[k]
        a, b = total[:HALF], total[HALF : 2 * HALF]
        o_ref[:, 0, k, :] = jnp.concatenate([a[:, :HALF], b[:, :HALF]], axis=1)
        o_ref[:, 1, k, :] = jnp.concatenate([a[:, HALF:], b[:, HALF:]], axis=1)
        o_ref[:, 2, k, :] = total[2 * HALF :]


def source_pack(kept, far, scale, others):
    bins = kept.shape[0]
    return call(
        source_pack_kernel,
        jax.ShapeDtypeStruct((HALF, 3, bins, 2 * HALF), F32),
        [vmem()] * (3 + len(others)),
        0,
        16 * kept.size,
    )(kept, far, scale, *others)


def source_rows(both, bins, k, i, unit):
    cut = slice(i * HALF, (i + 1) * HALF)
    return jnp.concatenate([both[k][:, cut], both[bins + k][:, cut]], axis=1) * unit


def source_unpack_kernel(x_ref, unit_ref, m_ref):
    bins, width = x_ref.shape[1] // 2, m_ref.shape[1]
    unit = unit_ref[0:1, :]
    both = jnp.transpose(x_ref[...], (1, 0, 2))
    norm = jnp.max(jnp.max(x_ref[:, 0, 3 * HALF :], axis=0, keepdims=True))
    at = 0
    for k in range(bins):
        for i in range(3):
            m_ref[at : at + HALF, :] = source_rows(both, bins, k, i, unit).astype(BF16)
            at += HALF
    m_ref[at:, :] = jnp.full((16, width), norm, F32).astype(BF16)


def source_unpack(x, unit):
    out = jax.ShapeDtypeStruct((x.shape[1] // 2 * 3 * HALF + 16, 2 * HALF), BF16)
    return call(source_unpack_kernel, out, [vmem()] * 2, 0, 6 * x.size)(x, unit)


def source_output_kernel(x_ref, unit_ref, o_ref):
    bins = x_ref.shape[1] // 2
    unit = unit_ref[0:1, :]
    both = jnp.transpose(x_ref[...], (1, 0, 2))
    for k in range(bins):
        for i in range(3):
            o_ref[i * HALF : (i + 1) * HALF, k, :] = source_rows(both, bins, k, i, unit)


def source_output(x, unit):
    out = jax.ShapeDtypeStruct((3 * HALF, x.shape[1] // 2, 2 * HALF), F32)
    return call(source_output_kernel, out, [vmem(), vmem()], 0, 8 * x.size)(x, unit)


def onset_kernel(order_ref, src_ref, rec_ref, src_row_ref, rec_row_ref):
    freq, first = order_ref[4], order_ref[5]
    lane = lax.broadcasted_iota(jnp.int32, src_ref.shape, 1)
    src = src_ref[...].astype(F32)
    rows = []
    for i in range(3):
        picked = jnp.where(lane == first + i * HALF + freq, src, 0.0)
        picked = jnp.sum(picked, axis=1, keepdims=True)
        rows.append(jnp.broadcast_to(picked, (HALF, 2 * HALF)).T[0:1, :])
    rows.append(jnp.zeros_like(rows[0]))
    src_row_ref[...] = jnp.concatenate(rows, axis=1).astype(jnp.int32)
    rec_row_ref[...] = rec_ref[pl.ds(freq, 1), :]


def onset_rows(order, src, rec):
    out = [jax.ShapeDtypeStruct((1, 4 * HALF), jnp.int32), jax.ShapeDtypeStruct((1, rec.shape[1]), jnp.int32)]
    return call(onset_kernel, out, [smem(), vmem(), vmem()], 0, 4 * (src.size + rec.size))(order, src, rec)


def plus_forward_kernel(picks, order_ref, r_ref, back_ref, init_ref, unit_ref, x_ref, *outs):
    bins, _, recs = init_ref.shape
    unit = jnp.max(unit_ref[...])
    both = jnp.transpose(back_ref[...], (1, 0, 2))
    for k in range(bins):
        rows = jnp.concatenate([both[k], both[bins + k]], axis=0) * unit
        x_ref[k] = (init_ref[k].astype(F32) + rows).astype(BF16)
        forward_bin(picks, order_ref, r_ref, x_ref, outs, k)


def plus_forward(order, response, back, init, unit, picks):
    bins, width, recs = init.shape
    block = response.shape[2] // 4
    return call(
        lambda *refs: plus_forward_kernel(picks, *refs),
        [jax.ShapeDtypeStruct(init.shape, BF16)] + [jax.ShapeDtypeStruct((bins, block, width), F32)] * len(picks),
        [smem()] + [vmem()] * 4,
        4 * bins * len(picks) * block * recs * width,
        4 * bins * len(picks) * block * recs,
    )(order, response, back, init, unit)


def final_kernel(x_ref, init_ref, unit_ref, o_ref, held_ref, sems):
    bins, _, recs = init_ref.shape
    unit = jnp.max(unit_ref[...])
    pieces = sems.shape[0]
    size = recs // pieces
    copies = []
    for i in range(pieces):
        cut = slice(i * size, (i + 1) * size)
        both = jnp.transpose(x_ref[:, :, cut], (1, 0, 2))
        for k in range(bins):
            rows = jnp.concatenate([both[k], both[bins + k]], axis=0) * unit
            held_ref[cut, k, :] = (init_ref[k][:, cut].astype(F32) + rows).T
        copies.append(pltpu.make_async_copy(held_ref.at[cut], o_ref.at[cut], sems.at[i]))
        copies[-1].start()
    for copy in copies:
        copy.wait()


def final_call(x, init, unit):
    bins, width, recs = init.shape
    out = jax.ShapeDtypeStruct((recs, bins, width), F32)
    return pl.pallas_call(
        final_kernel,
        in_specs=[vmem()] * 3,
        out_specs=pl.BlockSpec(memory_space=pl.ANY),
        out_shape=out,
        scratch_shapes=[pltpu.VMEM(out.shape, F32), pltpu.SemaphoreType.DMA((3,))],
        compiler_params=pltpu.CompilerParams(vmem_limit_bytes=16 * MIB),
        cost_estimate=pl.CostEstimate(flops=0, bytes_accessed=8 * x.size, transcendentals=0),
    )(x, init, unit)


def body(response, focus_init, onset_src, onset_rec):
    nfreq = lax.axis_size("freq")
    freq_pos = lax.axis_index("freq")
    rec_pos = lax.axis_index("rec")
    _, bins, sources, recs = response.shape
    width = focus_init.shape[2]
    block = sources // 4
    core, high = rec_pos % 2, rec_pos // 2
    tables = [jnp.asarray(t) for t in fold_tables(bins * nfreq)]

    def place(h, c):
        return h * 2 + c

    order = jnp.stack(
        [
            place(1 - high, 1 - core),
            place(1 - high, core),
            place(high, 1 - core),
            place(high, core),
            freq_pos,
            rec_pos * block,
        ]
    ).astype(jnp.int32)

    def swap(values):
        return lax.all_to_all(values.astype(F16), "freq", split_axis=0, concat_axis=0, tiled=True).astype(F32)

    def step_to(values, pairs):
        return lax.ppermute(values, "rec", pairs)

    init_norm = math.sqrt(2.0 * bins * nfreq) * INIT_ABS
    rec_gain = 4 * recs * R_ABS

    init_t = jnp.transpose(focus_init, (1, 2, 0))
    init_t, order = lax.optimization_barrier((init_t, order))
    src_onsets = rec_onsets = None
    plus = init_t
    bound = jnp.full((1, 128), rec_gain * init_norm, F32)
    scale, unit = TOP / bound, bound * (1.0 / TOP)
    minus_out = None
    plus_out = None
    for step in range(ITERS):
        last = step == ITERS - 1
        aside = None
        if step == 0:
            (away,) = forward_call(order, response, plus, (0,))
        else:
            plus, away, aside = plus_forward(order, response, back, init_t, back_unit, (0, 2))
        away = step_to(away, CORE_SWAP)
        (mine,) = forward_call(order, response, plus, (1,))
        coded = ((mine + away) * scale).astype(F16)
        if step == 0:
            coded, plus, late = lax.optimization_barrier((coded, plus, order))
            far = step_to(coded, HIGH_SWAP)
            aside, near = forward_call(order, response, plus, (2, 3))
            aside = [step_to(aside[k], CORE_SWAP) for k in range(bins)]
            src_onsets, rec_onsets = onset_rows(late, onset_src.T, onset_rec.T)
        else:
            coded, plus, aside = lax.optimization_barrier((coded, plus, aside))
            far = step_to(coded, HIGH_SWAP)
            aside = [step_to(aside, CORE_SWAP)]
            (near,) = forward_call(order, response, plus, (3,))
        far, src_onsets, rec_onsets = lax.optimization_barrier((far, src_onsets, rec_onsets))
        field = source_pack(near, far.astype(F32), scale, aside)
        field = swap(field).reshape(3 * HALF * bins, width)
        field = window_call(field, src_onsets, tables, True)
        field = swap(field)
        mine = source_unpack(field, unit)
        across = step_to(mine, HIGH_SWAP)
        beside = step_to(mine, CORE_SWAP)
        total = adjoint_first(order, response, mine, beside)
        if last:
            minus_out = source_output(field, unit)
            across, total, minus_out = lax.optimization_barrier((across, total, minus_out))
        else:
            across, total = lax.optimization_barrier((across, total))
        corner = step_to(across, CORE_SWAP)
        total = adjoint_middle(order, response, total, across)
        parts = (mine, beside, across, corner)
        behind, back_unit, scale, unit = adjoint_last(order, response, total, unit, parts, rec_gain, init_norm)
        field = window_call(swap(behind), rec_onsets, tables, False)
        back = swap(field)
        if last:
            plus_out = final_call(back, init_t, back_unit)
    return (minus_out, plus_out)


def solution(mesh):
    return jax.shard_map(
        body,
        mesh=mesh,
        in_specs=(P(None, "freq", None, "rec"), P("rec", "freq", None), P(), P("rec", None)),
        out_specs=(P("rec", "freq", None), P("rec", "freq", None)),
        check_vma=False,
    )
```

```python
import math

import jax
import jax.numpy as jnp
import numpy as np
from jax import lax
from jax.experimental import pallas as pl
from jax.experimental.pallas import tpu as pltpu
from jax.sharding import PartitionSpec as P

NT = 640
ITERS = 2
HALF = 64
FOLD = 336
R_ABS = 0.078125 * math.sqrt(2.0) * 1.001
INIT_ABS = 6.0
TOP = 16384.0
FLOOR = 2.0 ** -14
MIB = 1024 * 1024
F32 = jnp.float32
BF16 = jnp.bfloat16
F16 = jnp.float16

CORE_SWAP = [(0, 1), (1, 0), (2, 3), (3, 2)]
HIGH_SWAP = [(0, 2), (2, 0), (1, 3), (3, 1)]


def vmem():
    return pl.BlockSpec(memory_space=pltpu.VMEM)


def smem():
    return pl.BlockSpec(memory_space=pltpu.SMEM)


def call(kernel, out_shape, specs, flops, moved, limit=8):
    return pl.pallas_call(
        kernel,
        in_specs=specs,
        out_specs=jax.tree.map(lambda _: vmem(), out_shape),
        out_shape=out_shape,
        compiler_params=pltpu.CompilerParams(vmem_limit_bytes=limit * MIB),
        cost_estimate=pl.CostEstimate(flops=flops, bytes_accessed=moved, transcendentals=0),
    )


def high_low(values):
    values = np.asarray(values, np.float32)
    high = values.astype(jnp.bfloat16)
    return [high, (values - high.astype(np.float32)).astype(jnp.bfloat16)]


def three(values):
    high, low = high_low(values)
    return np.concatenate([high, high, low], axis=1)


def fold_tables(nbins):
    bins = np.arange(nbins, dtype=np.int64) + 1
    samples = np.arange(FOLD, dtype=np.int64)
    angles = ((bins[:, None] * samples[None, :]) % NT).astype(np.float64) * (2.0 * math.pi / NT)
    used = samples[None, :] <= NT // 2
    cosine = np.where(used, np.cos(angles), 0.0)
    sine = np.where(used, np.sin(angles), 0.0)
    forward = np.stack([three(cosine), three(sine)])
    inverse = np.stack([three(cosine.T * (2.0 / NT)), three(sine.T * (2.0 / NT))])
    return forward, inverse


def split_dot(table, x):
    high = x.astype(BF16)
    low = (x - high.astype(F32)).astype(BF16)
    return jnp.dot(table, jnp.concatenate([high, low, high], axis=0), preferred_element_type=F32)


def pair_halves(x_ref, first):
    blocks, _, lanes = x_ref.shape
    x = x_ref[...].reshape(blocks // 2, 2, 8, lanes)
    even, odd = x[:, 0], x[:, 1]
    real = jnp.where(first, even, pltpu.roll(odd, 4, 1))
    imag = jnp.where(first, pltpu.roll(even, 4, 1), odd)
    return real.reshape(blocks * 4, lanes), imag.reshape(blocks * 4, lanes)


def triple_halves(x_ref, first):
    groups = x_ref.shape[0] // 24
    x = x_ref[...].reshape(groups, 3, 8, 2 * HALF)
    a, b, c = x[:, 0], x[:, 1], x[:, 2]
    first = first[:, :, : 2 * HALF]
    real = jnp.where(first, a, b).reshape(groups * 8, 2 * HALF)
    imag = pltpu.roll(jnp.where(first, c, a), 4, 1).reshape(groups * 8, 2 * HALF)
    rest = jnp.where(first, b, c).reshape(groups * 8, 2 * HALF)
    return jnp.concatenate([real, rest], axis=1), jnp.concatenate([imag, pltpu.roll(rest, HALF, 1)], axis=1)


def window_kernel(from_source, x_ref, onset_ref, forward_ref, inverse_ref, o_ref):
    blocks, _, lanes = o_ref.shape
    first = lax.broadcasted_iota(jnp.int32, (blocks // 2, 8, lanes), 1) < 4
    real, imag = triple_halves(x_ref, first) if from_source else pair_halves(x_ref, first)
    a = split_dot(inverse_ref[0], real)
    b = split_dot(inverse_ref[1], imag)
    n = lax.broadcasted_iota(jnp.int32, a.shape, 0)
    onset = onset_ref[...]
    near = jnp.where(n < onset, a - b, 0.0)
    far = jnp.where((NT - n < onset) & (n > 0) & (n < NT // 2), a + b, 0.0)
    real = split_dot(forward_ref[0], near + far)
    imag = split_dot(forward_ref[1], far - near)
    norm = None
    if from_source:
        norm = jnp.sqrt(jnp.max(jnp.sum(real * real + imag * imag, axis=0, keepdims=True))) * 1.01
    real = real.reshape(blocks // 2, 8, lanes)
    imag = imag.reshape(blocks // 2, 8, lanes)
    even = jnp.where(first, real, pltpu.roll(imag, 4, 1))
    odd = jnp.where(first, pltpu.roll(real, 4, 1), imag)
    if from_source:
        spare = lax.broadcasted_iota(jnp.int32, even.shape, 2) >= 3 * HALF
        even = jnp.where(spare, norm, even)
        odd = jnp.where(spare, norm, odd)
    o_ref[...] = jnp.concatenate([even[:, None], odd[:, None]], axis=1).reshape(blocks, 8, lanes)


def window_call(x, onsets, tables, from_source):
    lanes = onsets.shape[1]
    blocks = x.shape[0] // 12 if from_source else x.shape[0]
    return call(
        lambda *refs: window_kernel(from_source, *refs),
        jax.ShapeDtypeStruct((blocks, 8, lanes), F32),
        [vmem()] * 4,
        12 * FOLD * 512 * lanes,
        2 * 4 * x.size,
        16,
    )(x, onsets, *tables)


def forward_bin(picks, order_ref, r_ref, x_ref, outs, k):
    block = outs[0].shape[1]
    dims = (((1,), (1,)), ((), ()))
    x = x_ref[k]
    y = jnp.concatenate([-x[HALF:], x[:HALF]], axis=0)
    starts = [pl.multiple_of(order_ref[pick] * block, HALF) for pick in picks]
    real = jnp.concatenate([r_ref[0, k, pl.ds(at, block), :] for at in starts], axis=0)
    imag = jnp.concatenate([r_ref[1, k, pl.ds(at, block), :] for at in starts], axis=0)
    both = lax.dot_general(real, x, dims, preferred_element_type=F32)
    both = both + lax.dot_general(imag, y, dims, preferred_element_type=F32)
    for i, o_ref in enumerate(outs):
        o_ref[k] = both[i * block : (i + 1) * block]


def forward_kernel(picks, order_ref, r_ref, x_ref, *outs):
    for k in range(x_ref.shape[0]):
        forward_bin(picks, order_ref, r_ref, x_ref, outs, k)


def forward_call(order, response, plus, picks):
    _, bins, sources, recs = response.shape
    width = plus.shape[1]
    block = sources // 4
    return call(
        lambda *refs: forward_kernel(picks, *refs),
        [jax.ShapeDtypeStruct((bins, block, width), F32)] * len(picks),
        [smem(), vmem(), vmem()],
        4 * bins * len(picks) * block * recs * width,
        4 * bins * len(picks) * block * recs,
    )(order, response, plus)


def adjoint_sum(order_ref, picks, r_ref, parts, k):
    block = r_ref.shape[2] // 4
    m = jnp.concatenate([part[k * block : (k + 1) * block, :] for part in parts], axis=0).T
    n = jnp.concatenate([m[HALF:], -m[:HALF]], axis=0)
    starts = [pl.multiple_of(order_ref[pick] * block, HALF) for pick in picks]
    real = jnp.concatenate([r_ref[0, k, pl.ds(at, block), :] for at in starts], axis=0)
    imag = jnp.concatenate([r_ref[1, k, pl.ds(at, block), :] for at in starts], axis=0)
    return jnp.dot(m, real, preferred_element_type=F32) + jnp.dot(n, imag, preferred_element_type=F32)


def adjoint_first_kernel(order_ref, r_ref, a_ref, b_ref, o_ref):
    for k in range(r_ref.shape[1]):
        o_ref[k] = adjoint_sum(order_ref, (3, 2), r_ref, (a_ref, b_ref), k)


def adjoint_first(order, response, mine, beside):
    _, bins, sources, recs = response.shape
    width = mine.shape[1]
    return call(
        adjoint_first_kernel,
        jax.ShapeDtypeStruct((bins, width, recs), F32),
        [smem()] + [vmem()] * 3,
        2 * bins * sources * recs * width,
        2 * bins * sources * recs,
    )(order, response, mine, beside)


def adjoint_middle_kernel(order_ref, r_ref, total_ref, part_ref, o_ref):
    for k in range(r_ref.shape[1]):
        o_ref[k] = total_ref[k] + adjoint_sum(order_ref, (1,), r_ref, (part_ref,), k)


def adjoint_middle(order, response, total, part):
    _, bins, sources, recs = response.shape
    return call(
        adjoint_middle_kernel,
        jax.ShapeDtypeStruct(total.shape, F32),
        [smem()] + [vmem()] * 3,
        bins * sources * recs * total.shape[1],
        bins * sources * recs,
    )(order, response, total, part)


def adjoint_last_kernel(
    gain,
    rec_gain,
    init_norm,
    order_ref,
    r_ref,
    total_ref,
    unit_ref,
    a_ref,
    b_ref,
    c_ref,
    d_ref,
    o_ref,
    back_ref,
    next_scale_ref,
    next_unit_ref,
):
    bins = r_ref.shape[1]
    block = r_ref.shape[2] // 4
    recs = r_ref.shape[3]
    peak = a_ref[bins * block :, :]
    for part in (b_ref, c_ref, d_ref):
        peak = jnp.maximum(peak, part[bins * block :, :])
    norm = jnp.maximum(jnp.max(peak.astype(F32), axis=0, keepdims=True), FLOOR)
    norm = jnp.broadcast_to(norm * (1.01 * 1.01 * gain), unit_ref.shape) * unit_ref[...]
    back_ref[...] = norm * (1.0 / TOP)
    after = rec_gain * (init_norm + norm)
    next_scale_ref[...] = TOP / after
    next_unit_ref[...] = after * (1.0 / TOP)
    scale = jnp.max(TOP / norm)
    real, imag = [], []
    for k in range(bins):
        both = total_ref[k] + adjoint_sum(order_ref, (0,), r_ref, (d_ref,), k)
        both = both * scale
        real.append(both[:HALF][None])
        imag.append(both[HALF:][None])
    both = jnp.concatenate(real + imag, axis=0)
    o_ref[...] = jnp.transpose(both, (1, 0, 2))


def adjoint_last(order, response, total, unit, parts, rec_gain, init_norm):
    _, bins, sources, recs = response.shape
    width = total.shape[1]
    gain = sources * R_ABS
    stat = jax.ShapeDtypeStruct(unit.shape, F32)
    return call(
        lambda *refs: adjoint_last_kernel(gain, rec_gain, init_norm, *refs),
        (jax.ShapeDtypeStruct((HALF, 2 * bins, recs), F32), stat, stat, stat),
        [smem()] + [vmem()] * 7,
        2 * bins * sources * recs * width,
        2 * bins * sources * recs,
    )(order, response, total, unit, *parts)


def source_pack_kernel(kept_ref, far_ref, scale_ref, *refs):
    others, o_ref = refs[:-1], refs[-1]
    bins = kept_ref.shape[0]
    scale = scale_ref[0:1, :]
    for k in range(bins):
        total = (kept_ref[k] + (others[0][k] if len(others) == 1 else others[k][...])) * scale + far_ref[k]
        a, b = total[:HALF], total[HALF : 2 * HALF]
        o_ref[:, 0, k, :] = jnp.concatenate([a[:, :HALF], b[:, :HALF]], axis=1)
        o_ref[:, 1, k, :] = jnp.concatenate([a[:, HALF:], b[:, HALF:]], axis=1)
        o_ref[:, 2, k, :] = total[2 * HALF :]


def source_pack(kept, far, scale, others):
    bins = kept.shape[0]
    return call(
        source_pack_kernel,
        jax.ShapeDtypeStruct((HALF, 3, bins, 2 * HALF), F32),
        [vmem()] * (3 + len(others)),
        0,
        16 * kept.size,
    )(kept, far, scale, *others)


def source_rows(both, bins, k, i, unit):
    cut = slice(i * HALF, (i + 1) * HALF)
    return jnp.concatenate([both[k][:, cut], both[bins + k][:, cut]], axis=1) * unit


def source_unpack_kernel(x_ref, unit_ref, m_ref):
    bins, width = x_ref.shape[1] // 2, m_ref.shape[1]
    unit = unit_ref[0:1, :]
    both = jnp.transpose(x_ref[...], (1, 0, 2))
    norm = jnp.max(jnp.max(x_ref[:, 0, 3 * HALF :], axis=0, keepdims=True))
    at = 0
    for k in range(bins):
        for i in range(3):
            m_ref[at : at + HALF, :] = source_rows(both, bins, k, i, unit).astype(BF16)
            at += HALF
    m_ref[at:, :] = jnp.full((16, width), norm, F32).astype(BF16)


def source_unpack(x, unit):
    out = jax.ShapeDtypeStruct((x.shape[1] // 2 * 3 * HALF + 16, 2 * HALF), BF16)
    return call(source_unpack_kernel, out, [vmem()] * 2, 0, 6 * x.size)(x, unit)


def source_output_kernel(x_ref, unit_ref, o_ref):
    bins = x_ref.shape[1] // 2
    unit = unit_ref[0:1, :]
    both = jnp.transpose(x_ref[...], (1, 0, 2))
    for k in range(bins):
        for i in range(3):
            o_ref[i * HALF : (i + 1) * HALF, k, :] = source_rows(both, bins, k, i, unit)


def source_output(x, unit):
    out = jax.ShapeDtypeStruct((3 * HALF, x.shape[1] // 2, 2 * HALF), F32)
    return call(source_output_kernel, out, [vmem(), vmem()], 0, 8 * x.size)(x, unit)


def onset_kernel(order_ref, src_ref, rec_ref, src_row_ref, rec_row_ref):
    freq, first = order_ref[4], order_ref[5]
    lane = lax.broadcasted_iota(jnp.int32, src_ref.shape, 1)
    src = src_ref[...].astype(F32)
    rows = []
    for i in range(3):
        picked = jnp.where(lane == first + i * HALF + freq, src, 0.0)
        picked = jnp.sum(picked, axis=1, keepdims=True)
        rows.append(jnp.broadcast_to(picked, (HALF, 2 * HALF)).T[0:1, :])
    rows.append(jnp.zeros_like(rows[0]))
    src_row_ref[...] = jnp.concatenate(rows, axis=1).astype(jnp.int32)
    rec_row_ref[...] = rec_ref[pl.ds(freq, 1), :]


def onset_rows(order, src, rec):
    out = [jax.ShapeDtypeStruct((1, 4 * HALF), jnp.int32), jax.ShapeDtypeStruct((1, rec.shape[1]), jnp.int32)]
    return call(onset_kernel, out, [smem(), vmem(), vmem()], 0, 4 * (src.size + rec.size))(order, src, rec)


def plus_forward_kernel(picks, order_ref, r_ref, back_ref, init_ref, unit_ref, x_ref, *outs):
    bins, _, recs = init_ref.shape
    unit = jnp.max(unit_ref[...])
    both = jnp.transpose(back_ref[...], (1, 0, 2))
    for k in range(bins):
        rows = jnp.concatenate([both[k], both[bins + k]], axis=0) * unit
        x_ref[k] = (init_ref[k].astype(F32) + rows).astype(BF16)
        forward_bin(picks, order_ref, r_ref, x_ref, outs, k)


def plus_forward(order, response, back, init, unit, picks):
    bins, width, recs = init.shape
    block = response.shape[2] // 4
    return call(
        lambda *refs: plus_forward_kernel(picks, *refs),
        [jax.ShapeDtypeStruct(init.shape, BF16)] + [jax.ShapeDtypeStruct((bins, block, width), F32)] * len(picks),
        [smem()] + [vmem()] * 4,
        4 * bins * len(picks) * block * recs * width,
        4 * bins * len(picks) * block * recs,
    )(order, response, back, init, unit)


def final_kernel(x_ref, init_ref, unit_ref, o_ref, held_ref, sems):
    bins, _, recs = init_ref.shape
    unit = jnp.max(unit_ref[...])
    pieces = sems.shape[0]
    size = recs // pieces
    copies = []
    for i in range(pieces):
        cut = slice(i * size, (i + 1) * size)
        both = jnp.transpose(x_ref[:, :, cut], (1, 0, 2))
        for k in range(bins):
            rows = jnp.concatenate([both[k], both[bins + k]], axis=0) * unit
            held_ref[cut, k, :] = (init_ref[k][:, cut].astype(F32) + rows).T
        copies.append(pltpu.make_async_copy(held_ref.at[cut], o_ref.at[cut], sems.at[i]))
        copies[-1].start()
    for copy in copies:
        copy.wait()


def final_call(x, init, unit):
    bins, width, recs = init.shape
    out = jax.ShapeDtypeStruct((recs, bins, width), F32)
    return pl.pallas_call(
        final_kernel,
        in_specs=[vmem()] * 3,
        out_specs=pl.BlockSpec(memory_space=pl.ANY),
        out_shape=out,
        scratch_shapes=[pltpu.VMEM(out.shape, F32), pltpu.SemaphoreType.DMA((3,))],
        compiler_params=pltpu.CompilerParams(vmem_limit_bytes=16 * MIB),
        cost_estimate=pl.CostEstimate(flops=0, bytes_accessed=8 * x.size, transcendentals=0),
    )(x, init, unit)


def body(response, focus_init, onset_src, onset_rec):
    nfreq = lax.axis_size("freq")
    freq_pos = lax.axis_index("freq")
    rec_pos = lax.axis_index("rec")
    _, bins, sources, recs = response.shape
    width = focus_init.shape[2]
    block = sources // 4
    core, high = rec_pos % 2, rec_pos // 2
    tables = [jnp.asarray(t) for t in fold_tables(bins * nfreq)]

    def place(h, c):
        return h * 2 + c

    order = jnp.stack(
        [
            place(1 - high, 1 - core),
            place(1 - high, core),
            place(high, 1 - core),
            place(high, core),
            freq_pos,
            rec_pos * block,
        ]
    ).astype(jnp.int32)

    def swap(values):
        return lax.all_to_all(values.astype(F16), "freq", split_axis=0, concat_axis=0, tiled=True).astype(F32)

    def step_to(values, pairs):
        return lax.ppermute(values, "rec", pairs)

    init_norm = math.sqrt(2.0 * bins * nfreq) * INIT_ABS
    rec_gain = 4 * recs * R_ABS

    init_t = jnp.transpose(focus_init, (1, 2, 0))
    init_t, order = lax.optimization_barrier((init_t, order))
    src_onsets = rec_onsets = None
    plus = init_t
    bound = jnp.full((1, 128), rec_gain * init_norm, F32)
    scale, unit = TOP / bound, bound * (1.0 / TOP)
    minus_out = None
    plus_out = None
    for step in range(ITERS):
        last = step == ITERS - 1
        aside = None
        if step == 0:
            (away,) = forward_call(order, response, plus, (0,))
        else:
            plus, away, aside = plus_forward(order, response, back, init_t, back_unit, (0, 2))
        away = step_to(away, CORE_SWAP)
        (mine,) = forward_call(order, response, plus, (1,))
        coded = ((mine + away) * scale).astype(F16)
        if step == 0:
            coded, plus, late = lax.optimization_barrier((coded, plus, order))
            far = step_to(coded, HIGH_SWAP)
            aside, near = forward_call(order, response, plus, (2, 3))
            aside = [step_to(aside[k], CORE_SWAP) for k in range(bins)]
            src_onsets, rec_onsets = onset_rows(late, onset_src.T, onset_rec.T)
        else:
            coded, plus, aside = lax.optimization_barrier((coded, plus, aside))
            far = step_to(coded, HIGH_SWAP)
            aside = [step_to(aside, CORE_SWAP)]
            (near,) = forward_call(order, response, plus, (3,))
        far, src_onsets, rec_onsets = lax.optimization_barrier((far, src_onsets, rec_onsets))
        field = source_pack(near, far.astype(F32), scale, aside)
        field = swap(field).reshape(3 * HALF * bins, width)
        field = window_call(field, src_onsets, tables, True)
        field = swap(field)
        mine = source_unpack(field, unit)
        across = step_to(mine, HIGH_SWAP)
        beside = step_to(mine, CORE_SWAP)
        total = adjoint_first(order, response, mine, beside)
        if last:
            minus_out = source_output(field, unit)
            across, total, minus_out = lax.optimization_barrier((across, total, minus_out))
        else:
            across, total = lax.optimization_barrier((across, total))
        corner = step_to(across, CORE_SWAP)
        total = adjoint_middle(order, response, total, across)
        parts = (mine, beside, across, corner)
        behind, back_unit, scale, unit = adjoint_last(order, response, total, unit, parts, rec_gain, init_norm)
        field = window_call(swap(behind), rec_onsets, tables, False)
        back = swap(field)
        if last:
            plus_out = final_call(back, init_t, back_unit)
    return (minus_out, plus_out)


def solution(mesh):
    return jax.shard_map(
        body,
        mesh=mesh,
        in_specs=(P(None, "freq", None, "rec"), P("rec", "freq", None), P(), P("rec", None)),
        out_specs=(P("rec", "freq", None), P("rec", "freq", None)),
        check_vma=False,
    )
```

```python
import math

import jax
import jax.numpy as jnp
import numpy as np
from jax import lax
from jax.experimental import pallas as pl
from jax.experimental.pallas import tpu as pltpu
from jax.sharding import PartitionSpec as P

NT = 640
ITERS = 2
HALF = 64
FOLD = 336
R_ABS = 0.078125 * math.sqrt(2.0) * 1.001
INIT_ABS = 6.0
TOP = 16384.0
FLOOR = 2.0 ** -14
MIB = 1024 * 1024
F32 = jnp.float32
BF16 = jnp.bfloat16
F16 = jnp.float16

CORE_SWAP = [(0, 1), (1, 0), (2, 3), (3, 2)]
HIGH_SWAP = [(0, 2), (2, 0), (1, 3), (3, 1)]


def vmem():
    return pl.BlockSpec(memory_space=pltpu.VMEM)


def smem():
    return pl.BlockSpec(memory_space=pltpu.SMEM)


def call(kernel, out_shape, specs, flops, moved, limit=8):
    return pl.pallas_call(
        kernel,
        in_specs=specs,
        out_specs=jax.tree.map(lambda _: vmem(), out_shape),
        out_shape=out_shape,
        compiler_params=pltpu.CompilerParams(vmem_limit_bytes=limit * MIB),
        cost_estimate=pl.CostEstimate(flops=flops, bytes_accessed=moved, transcendentals=0),
    )


def high_low(values):
    values = np.asarray(values, np.float32)
    high = values.astype(jnp.bfloat16)
    return [high, (values - high.astype(np.float32)).astype(jnp.bfloat16)]


def three(values):
    high, low = high_low(values)
    return np.concatenate([high, high, low], axis=1)


def fold_tables(nbins):
    bins = np.arange(nbins, dtype=np.int64) + 1
    samples = np.arange(FOLD, dtype=np.int64)
    angles = ((bins[:, None] * samples[None, :]) % NT).astype(np.float64) * (2.0 * math.pi / NT)
    used = samples[None, :] <= NT // 2
    cosine = np.where(used, np.cos(angles), 0.0)
    sine = np.where(used, np.sin(angles), 0.0)
    forward = np.stack([three(cosine), three(sine)])
    inverse = np.stack([three(cosine.T * (2.0 / NT)), three(sine.T * (2.0 / NT))])
    return forward, inverse


def split_dot(table, x):
    high = x.astype(BF16)
    low = (x - high.astype(F32)).astype(BF16)
    return jnp.dot(table, jnp.concatenate([high, low, high], axis=0), preferred_element_type=F32)


def pair_halves(x_ref, first):
    blocks, _, lanes = x_ref.shape
    x = x_ref[...].reshape(blocks // 2, 2, 8, lanes)
    even, odd = x[:, 0], x[:, 1]
    real = jnp.where(first, even, pltpu.roll(odd, 4, 1))
    imag = jnp.where(first, pltpu.roll(even, 4, 1), odd)
    return real.reshape(blocks * 4, lanes), imag.reshape(blocks * 4, lanes)


def triple_halves(x_ref, first):
    groups = x_ref.shape[0] // 24
    x = x_ref[...].reshape(groups, 3, 8, 2 * HALF)
    a, b, c = x[:, 0], x[:, 1], x[:, 2]
    first = first[:, :, : 2 * HALF]
    real = jnp.where(first, a, b).reshape(groups * 8, 2 * HALF)
    imag = pltpu.roll(jnp.where(first, c, a), 4, 1).reshape(groups * 8, 2 * HALF)
    rest = jnp.where(first, b, c).reshape(groups * 8, 2 * HALF)
    return jnp.concatenate([real, rest], axis=1), jnp.concatenate([imag, pltpu.roll(rest, HALF, 1)], axis=1)


def window_kernel(from_source, x_ref, onset_ref, forward_ref, inverse_ref, o_ref):
    blocks, _, lanes = o_ref.shape
    first = lax.broadcasted_iota(jnp.int32, (blocks // 2, 8, lanes), 1) < 4
    real, imag = triple_halves(x_ref, first) if from_source else pair_halves(x_ref, first)
    a = split_dot(inverse_ref[0], real)
    b = split_dot(inverse_ref[1], imag)
    n = lax.broadcasted_iota(jnp.int32, a.shape, 0)
    onset = onset_ref[...]
    near = jnp.where(n < onset, a - b, 0.0)
    far = jnp.where((NT - n < onset) & (n > 0) & (n < NT // 2), a + b, 0.0)
    real = split_dot(forward_ref[0], near + far)
    imag = split_dot(forward_ref[1], far - near)
    norm = None
    if from_source:
        norm = jnp.sqrt(jnp.max(jnp.sum(real * real + imag * imag, axis=0, keepdims=True))) * 1.01
    real = real.reshape(blocks // 2, 8, lanes)
    imag = imag.reshape(blocks // 2, 8, lanes)
    even = jnp.where(first, real, pltpu.roll(imag, 4, 1))
    odd = jnp.where(first, pltpu.roll(real, 4, 1), imag)
    if from_source:
        spare = lax.broadcasted_iota(jnp.int32, even.shape, 2) >= 3 * HALF
        even = jnp.where(spare, norm, even)
        odd = jnp.where(spare, norm, odd)
    o_ref[...] = jnp.concatenate([even[:, None], odd[:, None]], axis=1).reshape(blocks, 8, lanes)


def window_call(x, onsets, tables, from_source):
    lanes = onsets.shape[1]
    blocks = x.shape[0] // 12 if from_source else x.shape[0]
    return call(
        lambda *refs: window_kernel(from_source, *refs),
        jax.ShapeDtypeStruct((blocks, 8, lanes), F32),
        [vmem()] * 4,
        12 * FOLD * 512 * lanes,
        2 * 4 * x.size,
        16,
    )(x, onsets, *tables)


def forward_bin(picks, order_ref, r_ref, x_ref, outs, k):
    block = outs[0].shape[1]
    dims = (((1,), (1,)), ((), ()))
    x = x_ref[k]
    y = jnp.concatenate([-x[HALF:], x[:HALF]], axis=0)
    starts = [pl.multiple_of(order_ref[pick] * block, HALF) for pick in picks]
    real = jnp.concatenate([r_ref[0, k, pl.ds(at, block), :] for at in starts], axis=0)
    imag = jnp.concatenate([r_ref[1, k, pl.ds(at, block), :] for at in starts], axis=0)
    both = lax.dot_general(real, x, dims, preferred_element_type=F32)
    both = both + lax.dot_general(imag, y, dims, preferred_element_type=F32)
    for i, o_ref in enumerate(outs):
        o_ref[k] = both[i * block : (i + 1) * block]


def forward_kernel(picks, order_ref, r_ref, x_ref, *outs):
    for k in range(x_ref.shape[0]):
        forward_bin(picks, order_ref, r_ref, x_ref, outs, k)


def forward_call(order, response, plus, picks):
    _, bins, sources, recs = response.shape
    width = plus.shape[1]
    block = sources // 4
    return call(
        lambda *refs: forward_kernel(picks, *refs),
        [jax.ShapeDtypeStruct((bins, block, width), F32)] * len(picks),
        [smem(), vmem(), vmem()],
        4 * bins * len(picks) * block * recs * width,
        4 * bins * len(picks) * block * recs,
    )(order, response, plus)


def adjoint_sum(order_ref, picks, r_ref, parts, k):
    block = r_ref.shape[2] // 4
    m = jnp.concatenate([part[k * block : (k + 1) * block, :] for part in parts], axis=0).T
    n = jnp.concatenate([m[HALF:], -m[:HALF]], axis=0)
    starts = [pl.multiple_of(order_ref[pick] * block, HALF) for pick in picks]
    real = jnp.concatenate([r_ref[0, k, pl.ds(at, block), :] for at in starts], axis=0)
    imag = jnp.concatenate([r_ref[1, k, pl.ds(at, block), :] for at in starts], axis=0)
    both = jnp.concatenate([real, imag], axis=0)
    return jnp.dot(jnp.concatenate([m, n], axis=1), both, preferred_element_type=F32)


def adjoint_first_kernel(order_ref, r_ref, a_ref, b_ref, o_ref):
    for k in range(r_ref.shape[1]):
        o_ref[k] = adjoint_sum(order_ref, (3, 2), r_ref, (a_ref, b_ref), k)


def adjoint_first(order, response, mine, beside):
    _, bins, sources, recs = response.shape
    width = mine.shape[1]
    return call(
        adjoint_first_kernel,
        jax.ShapeDtypeStruct((bins, width, recs), F32),
        [smem()] + [vmem()] * 3,
        2 * bins * sources * recs * width,
        2 * bins * sources * recs,
    )(order, response, mine, beside)


def adjoint_middle_kernel(order_ref, r_ref, total_ref, part_ref, o_ref):
    for k in range(r_ref.shape[1]):
        o_ref[k] = total_ref[k] + adjoint_sum(order_ref, (1,), r_ref, (part_ref,), k)


def adjoint_middle(order, response, total, part):
    _, bins, sources, recs = response.shape
    return call(
        adjoint_middle_kernel,
        jax.ShapeDtypeStruct(total.shape, F32),
        [smem()] + [vmem()] * 3,
        bins * sources * recs * total.shape[1],
        bins * sources * recs,
    )(order, response, total, part)


def adjoint_last_kernel(
    gain,
    rec_gain,
    init_norm,
    order_ref,
    r_ref,
    total_ref,
    unit_ref,
    a_ref,
    b_ref,
    c_ref,
    d_ref,
    o_ref,
    back_ref,
    next_scale_ref,
    next_unit_ref,
):
    bins = r_ref.shape[1]
    block = r_ref.shape[2] // 4
    recs = r_ref.shape[3]
    peak = a_ref[bins * block :, :]
    for part in (b_ref, c_ref, d_ref):
        peak = jnp.maximum(peak, part[bins * block :, :])
    norm = jnp.maximum(jnp.max(peak.astype(F32), axis=0, keepdims=True), FLOOR)
    norm = jnp.broadcast_to(norm * (1.01 * 1.01 * gain), unit_ref.shape) * unit_ref[...]
    back_ref[...] = norm * (1.0 / TOP)
    after = rec_gain * (init_norm + norm)
    next_scale_ref[...] = TOP / after
    next_unit_ref[...] = after * (1.0 / TOP)
    scale = jnp.max(TOP / norm)
    real, imag = [], []
    for k in range(bins):
        both = total_ref[k] + adjoint_sum(order_ref, (0,), r_ref, (d_ref,), k)
        both = both * scale
        real.append(both[:HALF][None])
        imag.append(both[HALF:][None])
    both = jnp.concatenate(real + imag, axis=0)
    o_ref[...] = jnp.transpose(both, (1, 0, 2))


def adjoint_last(order, response, total, unit, parts, rec_gain, init_norm):
    _, bins, sources, recs = response.shape
    width = total.shape[1]
    gain = sources * R_ABS
    stat = jax.ShapeDtypeStruct(unit.shape, F32)
    return call(
        lambda *refs: adjoint_last_kernel(gain, rec_gain, init_norm, *refs),
        (jax.ShapeDtypeStruct((HALF, 2 * bins, recs), F32), stat, stat, stat),
        [smem()] + [vmem()] * 7,
        2 * bins * sources * recs * width,
        2 * bins * sources * recs,
    )(order, response, total, unit, *parts)


def source_pack_kernel(kept_ref, far_ref, scale_ref, *refs):
    others, o_ref = refs[:-1], refs[-1]
    bins = kept_ref.shape[0]
    scale = scale_ref[0:1, :]
    for k in range(bins):
        total = (kept_ref[k] + (others[0][k] if len(others) == 1 else others[k][...])) * scale + far_ref[k]
        a, b = total[:HALF], total[HALF : 2 * HALF]
        o_ref[:, 0, k, :] = jnp.concatenate([a[:, :HALF], b[:, :HALF]], axis=1)
        o_ref[:, 1, k, :] = jnp.concatenate([a[:, HALF:], b[:, HALF:]], axis=1)
        o_ref[:, 2, k, :] = total[2 * HALF :]


def source_pack(kept, far, scale, others):
    bins = kept.shape[0]
    return call(
        source_pack_kernel,
        jax.ShapeDtypeStruct((HALF, 3, bins, 2 * HALF), F32),
        [vmem()] * (3 + len(others)),
        0,
        16 * kept.size,
    )(kept, far, scale, *others)


def source_rows(both, bins, k, i, unit):
    cut = slice(i * HALF, (i + 1) * HALF)
    return jnp.concatenate([both[k][:, cut], both[bins + k][:, cut]], axis=1) * unit


def source_unpack_kernel(x_ref, unit_ref, m_ref):
    bins, width = x_ref.shape[1] // 2, m_ref.shape[1]
    unit = unit_ref[0:1, :]
    both = jnp.transpose(x_ref[...], (1, 0, 2))
    norm = jnp.max(jnp.max(x_ref[:, 0, 3 * HALF :], axis=0, keepdims=True))
    at = 0
    for k in range(bins):
        for i in range(3):
            m_ref[at : at + HALF, :] = source_rows(both, bins, k, i, unit).astype(BF16)
            at += HALF
    m_ref[at:, :] = jnp.full((16, width), norm, F32).astype(BF16)


def source_unpack(x, unit):
    out = jax.ShapeDtypeStruct((x.shape[1] // 2 * 3 * HALF + 16, 2 * HALF), BF16)
    return call(source_unpack_kernel, out, [vmem()] * 2, 0, 6 * x.size)(x, unit)


def source_output_kernel(x_ref, unit_ref, o_ref):
    bins = x_ref.shape[1] // 2
    unit = unit_ref[0:1, :]
    both = jnp.transpose(x_ref[...], (1, 0, 2))
    for k in range(bins):
        for i in range(3):
            o_ref[i * HALF : (i + 1) * HALF, k, :] = source_rows(both, bins, k, i, unit)


def source_output(x, unit):
    out = jax.ShapeDtypeStruct((3 * HALF, x.shape[1] // 2, 2 * HALF), F32)
    return call(source_output_kernel, out, [vmem(), vmem()], 0, 8 * x.size)(x, unit)


def onset_kernel(order_ref, src_ref, rec_ref, src_row_ref, rec_row_ref):
    freq, first = order_ref[4], order_ref[5]
    lane = lax.broadcasted_iota(jnp.int32, src_ref.shape, 1)
    src = src_ref[...].astype(F32)
    rows = []
    for i in range(3):
        picked = jnp.where(lane == first + i * HALF + freq, src, 0.0)
        picked = jnp.sum(picked, axis=1, keepdims=True)
        rows.append(jnp.broadcast_to(picked, (HALF, 2 * HALF)).T[0:1, :])
    rows.append(jnp.zeros_like(rows[0]))
    src_row_ref[...] = jnp.concatenate(rows, axis=1).astype(jnp.int32)
    rec_row_ref[...] = rec_ref[pl.ds(freq, 1), :]


def onset_rows(order, src, rec):
    out = [jax.ShapeDtypeStruct((1, 4 * HALF), jnp.int32), jax.ShapeDtypeStruct((1, rec.shape[1]), jnp.int32)]
    return call(onset_kernel, out, [smem(), vmem(), vmem()], 0, 4 * (src.size + rec.size))(order, src, rec)


def plus_forward_kernel(picks, order_ref, r_ref, back_ref, init_ref, unit_ref, x_ref, *outs):
    bins, _, recs = init_ref.shape
    unit = jnp.max(unit_ref[...])
    both = jnp.transpose(back_ref[...], (1, 0, 2))
    for k in range(bins):
        rows = jnp.concatenate([both[k], both[bins + k]], axis=0) * unit
        x_ref[k] = (init_ref[k].astype(F32) + rows).astype(BF16)
        forward_bin(picks, order_ref, r_ref, x_ref, outs, k)


def plus_forward(order, response, back, init, unit, picks):
    bins, width, recs = init.shape
    block = response.shape[2] // 4
    return call(
        lambda *refs: plus_forward_kernel(picks, *refs),
        [jax.ShapeDtypeStruct(init.shape, BF16)] + [jax.ShapeDtypeStruct((bins, block, width), F32)] * len(picks),
        [smem()] + [vmem()] * 4,
        4 * bins * len(picks) * block * recs * width,
        4 * bins * len(picks) * block * recs,
    )(order, response, back, init, unit)


def final_kernel(x_ref, init_ref, unit_ref, o_ref, held_ref, sems):
    bins, _, recs = init_ref.shape
    unit = jnp.max(unit_ref[...])
    pieces = sems.shape[0]
    size = recs // pieces
    copies = []
    for i in range(pieces):
        cut = slice(i * size, (i + 1) * size)
        both = jnp.transpose(x_ref[:, :, cut], (1, 0, 2))
        for k in range(bins):
            rows = jnp.concatenate([both[k], both[bins + k]], axis=0) * unit
            held_ref[cut, k, :] = (init_ref[k][:, cut].astype(F32) + rows).T
        copies.append(pltpu.make_async_copy(held_ref.at[cut], o_ref.at[cut], sems.at[i]))
        copies[-1].start()
    for copy in copies:
        copy.wait()


def final_call(x, init, unit):
    bins, width, recs = init.shape
    out = jax.ShapeDtypeStruct((recs, bins, width), F32)
    return pl.pallas_call(
        final_kernel,
        in_specs=[vmem()] * 3,
        out_specs=pl.BlockSpec(memory_space=pl.ANY),
        out_shape=out,
        scratch_shapes=[pltpu.VMEM(out.shape, F32), pltpu.SemaphoreType.DMA((3,))],
        compiler_params=pltpu.CompilerParams(vmem_limit_bytes=16 * MIB),
        cost_estimate=pl.CostEstimate(flops=0, bytes_accessed=8 * x.size, transcendentals=0),
    )(x, init, unit)


def body(response, focus_init, onset_src, onset_rec):
    nfreq = lax.axis_size("freq")
    freq_pos = lax.axis_index("freq")
    rec_pos = lax.axis_index("rec")
    _, bins, sources, recs = response.shape
    width = focus_init.shape[2]
    block = sources // 4
    core, high = rec_pos % 2, rec_pos // 2
    tables = [jnp.asarray(t) for t in fold_tables(bins * nfreq)]

    def place(h, c):
        return h * 2 + c

    order = jnp.stack(
        [
            place(1 - high, 1 - core),
            place(1 - high, core),
            place(high, 1 - core),
            place(high, core),
            freq_pos,
            rec_pos * block,
        ]
    ).astype(jnp.int32)

    def swap(values):
        return lax.all_to_all(values.astype(F16), "freq", split_axis=0, concat_axis=0, tiled=True).astype(F32)

    def step_to(values, pairs):
        return lax.ppermute(values, "rec", pairs)

    init_norm = math.sqrt(2.0 * bins * nfreq) * INIT_ABS
    rec_gain = 4 * recs * R_ABS

    init_t = jnp.transpose(focus_init, (1, 2, 0))
    init_t, order = lax.optimization_barrier((init_t, order))
    src_onsets = rec_onsets = None
    plus = init_t
    bound = jnp.full((1, 128), rec_gain * init_norm, F32)
    scale, unit = TOP / bound, bound * (1.0 / TOP)
    minus_out = None
    plus_out = None
    for step in range(ITERS):
        last = step == ITERS - 1
        aside = None
        if step == 0:
            (away,) = forward_call(order, response, plus, (0,))
        else:
            plus, away, aside = plus_forward(order, response, back, init_t, back_unit, (0, 2))
        away = step_to(away, CORE_SWAP)
        (mine,) = forward_call(order, response, plus, (1,))
        coded = ((mine + away) * scale).astype(F16)
        if step == 0:
            coded, plus, late = lax.optimization_barrier((coded, plus, order))
            far = step_to(coded, HIGH_SWAP)
            aside, near = forward_call(order, response, plus, (2, 3))
            aside = [step_to(aside[k], CORE_SWAP) for k in range(bins)]
            src_onsets, rec_onsets = onset_rows(late, onset_src.T, onset_rec.T)
        else:
            coded, plus, aside = lax.optimization_barrier((coded, plus, aside))
            far = step_to(coded, HIGH_SWAP)
            aside = [step_to(aside, CORE_SWAP)]
            (near,) = forward_call(order, response, plus, (3,))
        far, src_onsets, rec_onsets = lax.optimization_barrier((far, src_onsets, rec_onsets))
        field = source_pack(near, far.astype(F32), scale, aside)
        field = swap(field).reshape(3 * HALF * bins, width)
        field = window_call(field, src_onsets, tables, True)
        field = swap(field)
        mine = source_unpack(field, unit)
        across = step_to(mine, HIGH_SWAP)
        beside = step_to(mine, CORE_SWAP)
        total = adjoint_first(order, response, mine, beside)
        if last:
            minus_out = source_output(field, unit)
            across, total, minus_out = lax.optimization_barrier((across, total, minus_out))
        else:
            across, total = lax.optimization_barrier((across, total))
        corner = step_to(across, CORE_SWAP)
        total = adjoint_middle(order, response, total, across)
        parts = (mine, beside, across, corner)
        behind, back_unit, scale, unit = adjoint_last(order, response, total, unit, parts, rec_gain, init_norm)
        field = window_call(swap(behind), rec_onsets, tables, False)
        back = swap(field)
        if last:
            plus_out = final_call(back, init_t, back_unit)
    return (minus_out, plus_out)


def solution(mesh):
    return jax.shard_map(
        body,
        mesh=mesh,
        in_specs=(P(None, "freq", None, "rec"), P("rec", "freq", None), P(), P("rec", None)),
        out_specs=(P("rec", "freq", None), P("rec", "freq", None)),
        check_vma=False,
    )
```
